32 devices in a mesh: groups: 2 (over y), expert: 8 (over z, core), beam: 2 (over x), head: 1.
Axes of the slice: x: 2, y: 2, z: 4, core: 2. Of those that a mesh axis runs over, the one named last changes fastest.
Arguments:
- states: bfloat16 [8, 4, 32, 128, 128], P('expert', ('groups', 'beam'), 'head'), parts along dimension 1, may hold values from -6 to 6
- qkv_rows: bfloat16 [3, 8, 4, 32, 128], P(None, 'expert', ('groups', 'beam'), 'head'), parts along dimension 2, may hold values from -6 to 6
- decay_rate: float32 [8, 4, 32], P('expert', ('groups', 'beam'), 'head'), parts along dimension 1, may hold values from 0.05 to 1
- parents: int32 [8, 4], P(None, ('groups', 'beam')), parts along dimension 1, may hold values from 0 to 7, as said below
- hidden: bfloat16 [8, 4, 3072], P('expert', ('groups', 'beam')), parts along dimension 1, may hold values from -6 to 6
- expert_ids: int32 [8, 4, 2], P('expert', 'groups'), parts along dimension 1, may hold values from 0 to 3, all different within a row; in each aligned block of 2 rows (0 to 1, 2 to 3, ..., all dimensions but the last counted through in order) at most 2 rows name the same one
- gate_weights: float32 [8, 4, 2], P('expert', 'groups'), parts along dimension 1, may hold values from 0.1 to 1
- w_gate: bfloat16 [8, 3072, 2304], P('expert', None, ('beam', 'head')), may hold values from -0.109375 to 0.109375
- w_up: bfloat16 [8, 3072, 2304], P('expert', None, ('beam', 'head')), may hold values from -0.109375 to 0.109375
- w_down: bfloat16 [8, 2304, 3072], P('expert', ('beam', 'head')), may hold values from -0.09375 to 0.09375
Outputs:
- new_states: bfloat16 [8, 4, 32, 128, 128], P('expert', ('groups', 'beam'), 'head'), parts along dimension 1
- readout: bfloat16 [8, 4, 32, 128], P('expert', ('groups', 'beam'), 'head'), parts along dimension 1
- mixed: bfloat16 [8, 4, 3072], P('expert', ('groups', 'beam'), 'head'), parts along dimension 1
The draws below stay inside these ranges and needn't reach their ends.
There are 2 independent parts, one for each index of `groups`. The reference program is written for one: setup_inputs(seed, part) draws one part's arguments, and reference() takes and returns one part's arrays. A program takes and returns all parts, laid end to end along the dimension named above; an argument that names none is the same for every part. Nothing has to cross between parts.
Inputs may be any that keep to these rules, and one draw needn't show every extreme that they name: For every request, the 8 beams name exactly 4 distinct parents. `expert_ids`: each row names 2 different experts; among the 2 rows of one beam (aligned blocks of 2 rows) no expert is named by more than 2 rows.
All inputs are finite; a program needn't handle non-finite values.
Results may differ from the reference program's by a relative error of at most 0.0049.
Values may be sent and summed in bfloat16 or wider, within the bound.
A program may use at most 64 MiB of HBM per device.

```python
import math
import jax
import jax.numpy as jnp
import numpy as np
from jax import lax

D = 3072
FF = 4608
HEADS = 32
HEAD_DIM = 128
TOP = 2
PAR = 4
REQ = 2
BEAMS = 8
EXPERTS = 4
CAP = 2


def draw_parents(key, part):
    key = jax.random.fold_in(key, 7)
    key_first, key_pick, key_order = jax.random.split(key, 3)
    first_keys = jax.random.split(key_first, REQ)
    shuffled = jax.vmap(lambda single: jax.random.permutation(single, BEAMS))(first_keys).astype(jnp.int32)
    distinct = shuffled[:, :PAR]
    picks = jax.random.randint(key_pick, (REQ, BEAMS), 0, PAR).astype(jnp.int32)
    seeded = jnp.concatenate([jnp.broadcast_to(jnp.arange(PAR, dtype=jnp.int32), (REQ, PAR)), picks[:, PAR:]], axis=1)
    order_keys = jax.random.split(key_order, REQ)
    orders = jax.vmap(lambda single: jax.random.permutation(single, BEAMS))(order_keys).astype(jnp.int32)
    placed = jnp.take_along_axis(seeded, orders, axis=1)
    parent_map = jnp.take_along_axis(distinct, placed, axis=1)
    return parent_map.T.astype(jnp.int32)


def steps_of(rng, extent, cuts, low, high):
    def one(dim, shards_of):
        steps = jax.random.uniform(jax.random.fold_in(jax.random.fold_in(rng, 6), dim), (shards_of,), jnp.float32, low / len(cuts), high / len(cuts))
        return jnp.repeat(jnp.exp(steps), extent[dim] // shards_of).reshape((-1,) + (1,) * (len(extent) - dim - 1))

    factor_of = one(*cuts[0])
    for cut in cuts[1:]:
        factor_of = factor_of * one(*cut)
    return factor_of


def routed_block(stream_key, own, number, rows, amount, top, limit, skew):
    order = jax.random.permutation(stream_key, amount)
    packed, usual = shares(amount, rows * top, limit, skew, True), shares(amount, rows * top, limit, skew, False)
    places = jnp.arange(amount)

    def named(tallies, rotation):
        used = int((tallies > 0).sum())
        fixed = max(1, used // 4)
        passed = fixed + (places - fixed + rotation * (used - fixed)) % max(1, amount - fixed)
        return jnp.zeros((amount,), jnp.int32).at[order[jnp.where(places < fixed, places, passed)]].set(jnp.asarray(tallies, jnp.int32))

    tallies = jnp.where(number % 4 == 0, named(packed, number // 4), named(usual, number - number // 4 - 1))
    mixed = jax.random.permutation(jax.random.fold_in(own, 3), amount)
    giver, sink = mixed[0:amount // 2 * 2:2], mixed[1:amount // 2 * 2:2]
    margin = jnp.minimum(tallies[giver] - 1, limit - tallies[sink]) // 2
    margin = jnp.where((giver == order[0]) | (sink == order[0]) | (tallies[sink] == 0), 0, jnp.maximum(margin, 0))
    passed = jax.random.randint(jax.random.fold_in(own, 4), (amount // 2,), 0, 1 << 20) % (margin + 1)
    tallies = tallies.at[giver].add(-passed).at[sink].add(passed)
    labels = jnp.searchsorted(jnp.cumsum(tallies), jnp.arange(rows * top), side="right").astype(jnp.int32)
    table = labels.reshape(top, rows).T
    table = table[jax.random.permutation(jax.random.fold_in(own, 1), rows)]
    rotation = jax.random.randint(jax.random.fold_in(own, 2), (rows, 1), 0, top)
    return jnp.take_along_axis(table, (jnp.arange(top)[None, :] + rotation) % top, axis=1)


def shares(count, total, limit, lean, full):
    loads = [(1 << 20) // math.isqrt(grade ** lean) + 1 for grade in range(1, count + 1)]
    largest = limit if full else min(limit, max(-(-total // count), total * loads[0] // sum(loads)))
    least = 1 if total - largest >= count - 1 else 0
    holding, rest = [largest] + [least] * (count - 1), total - largest - least * (count - 1)
    while rest > 0:
        movable = [i for i in range(1, count) if holding[i] < largest] or [i for i in range(1, count) if holding[i] < limit]
        pool, budget = sum([loads[i] for i in movable]), rest
        for i in movable:
            extra = min(limit - holding[i], max(1, budget * loads[i] // pool), rest)
            holding[i] = holding[i] + extra
            rest = rest - extra
    return np.array(holding)


def bell_draw(own_key, dims, width, bound, cuts=(), kind=jnp.bfloat16):
    gain = steps_of(own_key, dims, cuts, -0.22, 0.18) if cuts else 1.0
    result = jax.random.normal(own_key, dims, jnp.float32) * width * gain
    return jnp.minimum(jnp.maximum(result, -bound), bound).astype(kind)


def setup_inputs(seed: int = 0, part: int = 0) -> dict:
    arg_keys = jax.random.split(jax.random.key(seed), 11)
    part_keys = jax.random.split(jax.random.fold_in(arg_keys[10], part), 11)
    states = bell_draw(part_keys[0], (BEAMS, REQ, HEADS, HEAD_DIM, HEAD_DIM), 1.0, 6.0, ((0, 8), (1, 2)))
    qkv_rows = bell_draw(part_keys[1], (3, BEAMS, REQ, HEADS, HEAD_DIM), 1.0, 6.0, ((1, 8), (2, 2)))
    decay_rate = jnp.clip(jnp.exp(math.log(1.0) - 2.9957323 * jax.random.uniform(part_keys[2], (BEAMS, REQ, HEADS), jnp.float32) ** steps_of(part_keys[2], (BEAMS, REQ, HEADS), ((0, 8), (1, 2)), -0.2, 0.2)), 0.05, 1.0)
    parents = draw_parents(jax.random.fold_in(jax.random.fold_in(arg_keys[10], part), 71), part)
    hidden = bell_draw(part_keys[4], (BEAMS, REQ, D), 1.0, 6.0, ((0, 8), (1, 2)))
    expert_ids_keys = jax.random.split(jax.random.fold_in(part_keys[5], 1), BEAMS * REQ // REQ)
    expert_ids_turns = jax.random.permutation(jax.random.fold_in(part_keys[5], 3), BEAMS * REQ // REQ)
    expert_ids = jax.vmap(lambda own, number: routed_block(jax.random.fold_in(part_keys[5], 2), own, number, REQ, EXPERTS, TOP, CAP, 2))(expert_ids_keys, expert_ids_turns).reshape((BEAMS, REQ, TOP))
    gate_weights = jnp.clip(0.1 + 0.9 * jax.random.uniform(part_keys[6], (BEAMS, REQ, TOP), jnp.float32) ** steps_of(part_keys[6], (BEAMS, REQ, TOP), ((0, 8),), -0.2, 0.2), 0.1, 1.0)
    w_gate = bell_draw(arg_keys[7], (2 * EXPERTS, D, FF // 2), D ** -0.5, 0.109375, ((0, 8), (2, 2)))
    w_up = bell_draw(arg_keys[8], (2 * EXPERTS, D, FF // 2), D ** -0.5, 0.109375, ((0, 8), (2, 2)))
    w_down = bell_draw(arg_keys[9], (2 * EXPERTS, FF // 2, D), FF ** -0.5, 0.09375, ((0, 8), (1, 2)))
    return {"states": states, "qkv_rows": qkv_rows, "decay_rate": decay_rate, "parents": parents, "hidden": hidden, "expert_ids": expert_ids, "gate_weights": gate_weights, "w_gate": w_gate, "w_up": w_up, "w_down": w_down}


def reference(states, qkv_rows, decay_rate, parents, hidden, expert_ids, gate_weights, w_gate, w_up, w_down):
    request_ids = jnp.arange(REQ, dtype=jnp.int32)
    parent_state = states[parents, request_ids[None, :]].astype(jnp.float32)
    query = qkv_rows[0].astype(jnp.float32)
    key_part = qkv_rows[1].astype(jnp.float32)
    value_part = qkv_rows[2].astype(jnp.float32)
    updated = decay_rate[..., None, None] * parent_state + key_part[..., :, None] * value_part[..., None, :]
    new_states = updated.astype(jnp.bfloat16)
    raw_out = jnp.einsum('brhk,brhkv->brhv', query, updated, precision=lax.Precision.HIGHEST)
    readout = (raw_out * lax.rsqrt(lax.optimization_barrier(jnp.mean(raw_out * raw_out, axis=-1, keepdims=True)) + 1e-05)).astype(jnp.bfloat16)
    flat_rows = hidden.reshape(BEAMS * REQ, D)
    flat_ids = expert_ids.reshape(BEAMS * REQ, TOP)
    flat_gates = gate_weights.reshape(BEAMS * REQ, TOP)
    expert_range = jnp.arange(EXPERTS, dtype=jnp.int32)
    coefficient = lax.optimization_barrier(jnp.sum(jnp.where(flat_ids[:, :, None] == expert_range[None, None, :], flat_gates[:, :, None], jnp.zeros((), jnp.float32)), axis=1))

    def expert_term(index):
        first_shard = (2 * index).astype(jnp.int32)
        gate_half = lax.dynamic_slice_in_dim(w_gate, first_shard, 2, 0)
        up_half = lax.dynamic_slice_in_dim(w_up, first_shard, 2, 0)
        down_half = lax.dynamic_slice_in_dim(w_down, first_shard, 2, 0)
        gate_full = jnp.concatenate([gate_half[0], gate_half[1]], axis=1)
        up_full = jnp.concatenate([up_half[0], up_half[1]], axis=1)
        down_full = jnp.concatenate([down_half[0], down_half[1]], axis=0)
        gate_val = jnp.dot(flat_rows, gate_full, preferred_element_type=jnp.float32)
        up_val = jnp.dot(flat_rows, up_full, preferred_element_type=jnp.float32)
        middle = (jax.nn.silu(gate_val) * up_val).astype(jnp.bfloat16)
        output = jnp.dot(middle, down_full, preferred_element_type=jnp.float32)
        weight_col = lax.dynamic_index_in_dim(coefficient, index, 1, keepdims=True)
        return output * weight_col
    terms = lax.map(expert_term, expert_range)
    mixed = lax.optimization_barrier(jnp.sum(terms, axis=0)).astype(jnp.bfloat16).reshape(BEAMS, REQ, D)
    return (new_states, readout, mixed)
```

```python
import jax
import jax.numpy as jnp
from jax import lax
from jax.experimental import pallas as pl
from jax.experimental.pallas import tpu as pltpu
from jax.sharding import PartitionSpec as P


def local(
    states, qkv_rows, decay_rate, parents, hidden, expert_ids, gate_weights, w_gate, w_up, w_down
):
    beam_index = lax.axis_index("expert")
    parent_ids = lax.dynamic_index_in_dim(parents, beam_index, 0, keepdims=False)
    shard_piece = lax.all_gather(states, "expert", axis=0, tiled=True)
    source_ids = jnp.arange(shard_piece.shape[0], dtype=jnp.int32)
    matches = source_ids[:, None] == parent_ids[None, :]
    chosen = jnp.sum(
        jnp.where(matches[:, :, None, None, None], shard_piece, jnp.zeros((), jnp.bfloat16)), axis=0
    )
    query = qkv_rows[0, 0].astype(jnp.float32)
    key_part = qkv_rows[1, 0].astype(jnp.float32)
    value_part = qkv_rows[2, 0].astype(jnp.float32)
    updated = (
        decay_rate[0][..., None, None] * chosen.astype(jnp.float32)
        + key_part[..., :, None] * value_part[..., None, :]
    )
    new_states = updated.astype(jnp.bfloat16)[None]
    raw_out = jnp.einsum("rhk,rhkv->rhv", query, updated, precision=lax.Precision.HIGHEST)
    readout = (
        raw_out * lax.rsqrt(jnp.mean(raw_out * raw_out, axis=-1, keepdims=True) + 1e-05)
    ).astype(jnp.bfloat16)[None]
    beam_block = lax.all_gather(hidden, "beam", axis=1, tiled=True)[0]
    route_ids = expert_ids[0]
    route_gates = gate_weights[0]
    request_count = beam_block.shape[0]
    top_count = route_ids.shape[1]
    expert_count = lax.axis_size("expert") // 2
    capacity = min(request_count, 2 * request_count * top_count // expert_count)
    expert_range = jnp.arange(expert_count, dtype=jnp.int32)
    flat_ids = route_ids.reshape(-1)
    one_hot = (flat_ids[None, :] == expert_range[:, None]).astype(jnp.int32)
    slot_rank = jnp.cumsum(one_hot, axis=1) - 1
    slot_range = jnp.arange(capacity, dtype=jnp.int32)
    assignment = one_hot[:, :, None] * (slot_rank[:, :, None] == slot_range[None, None, :]).astype(
        jnp.int32
    )
    placement = assignment.reshape(expert_count, request_count, top_count, capacity).sum(axis=2)
    gate_select = jnp.sum(
        jnp.where(
            route_ids[None, :, :] == expert_range[:, None, None],
            route_gates[None, :, :],
            jnp.zeros((), jnp.float32),
        ),
        axis=2,
    )
    combine_weight = placement.astype(jnp.float32) * gate_select[:, :, None]
    dispatched = jnp.einsum(
        "xrc,rd->xcd",
        placement.astype(jnp.bfloat16),
        beam_block,
        preferred_element_type=jnp.float32,
    ).astype(jnp.bfloat16)
    outgoing = jnp.repeat(dispatched, 2, axis=0)
    arrived = lax.all_to_all(outgoing, "expert", split_axis=0, concat_axis=0, tiled=True)
    gate_val = jnp.einsum("scd,df->scf", arrived, w_gate[0], preferred_element_type=jnp.float32)
    up_val = jnp.einsum("scd,df->scf", arrived, w_up[0], preferred_element_type=jnp.float32)
    middle = (jax.nn.silu(gate_val) * up_val).astype(jnp.bfloat16)
    partial_value = jnp.einsum("scf,fd->scd", middle, w_down[0], preferred_element_type=jnp.float32)
    returned = lax.all_to_all(partial_value, "expert", split_axis=0, concat_axis=0, tiled=True)
    paired = returned.reshape(expert_count, 2, capacity, returned.shape[2]).sum(axis=1)
    partial_rows = jnp.einsum(
        "xrc,xcd->rd", combine_weight, paired, precision=lax.Precision.HIGHEST
    )
    beam_size = lax.axis_size("beam")
    head_size = lax.axis_size("head")
    local_rows = request_count // beam_size
    model_width = partial_rows.shape[1]
    arranged = partial_rows.reshape(beam_size, local_rows, head_size, model_width // head_size)
    arranged = arranged.transpose(0, 2, 1, 3).reshape(
        beam_size * head_size * local_rows, model_width // head_size
    )
    summed = lax.psum_scatter(arranged, ("beam", "head"), scatter_dimension=0, tiled=True)
    mixed = summed.astype(jnp.bfloat16).reshape(1, local_rows, model_width // head_size)
    return (new_states, readout, mixed)


CHUNKS = 8
PIECES = 4
SUB = 8


def fused_kernel(
    parents, decay, ids, gates, qkv, hid, states, w_gate, w_up, w_down,
    new_states, readout, mixed,
    row, rows, xb, gate_acc, up_acc, part, part_in, summed, final, raw,
    wg, wu, wd, picked, fresh,
    row_send, row_recv, block_send, block_recv, part_send, part_recv, sum_send, sum_recv,
    w_sem, own_sem, out_sem, st_send, st_recv, fwd_send, pick_send,
    *cand,
):
    e = lax.axis_index("expert")
    be = lax.axis_index("beam")
    z, c = e // 2, e % 2
    q = c * 2 + be
    side = z // 2
    inner = (z == 1) | (z == 2)
    outer = (z == 0) | (z == 3)
    sib = z * 2 + (1 - c)
    near = (1 + side) * 2 + c
    far = (2 - side) * 2 + c
    edge = 3 * side * 2 + c
    far_edge = 3 * (1 - side) * 2 + c
    chunks = len(cand)
    heads = qkv.shape[3]
    hc = heads // chunks
    width = row.shape[1]
    depth, hidden_units = w_gate.shape[1], w_gate.shape[2]
    f32 = jnp.float32

    def flip(index):
        return index + 1 - 2 * c

    def remote(src, dst, ssem, rsem, expert, beam):
        return pltpu.make_async_remote_copy(
            src_ref=src, dst_ref=dst, send_sem=ssem, recv_sem=rsem,
            device_id={"expert": expert, "beam": beam}, device_id_type=pl.DeviceIdType.MESH,
        )

    barrier = pltpu.get_barrier_semaphore()
    for step in range(1, 16):
        other = (e * 2 + be + step) % 16
        pl.semaphore_signal(
            barrier, inc=1, device_id={"expert": other // 2, "beam": other % 2},
            device_id_type=pl.DeviceIdType.MESH,
        )

    for p in range(PIECES):
        span = pl.ds(p * (depth // PIECES), depth // PIECES)
        pltpu.make_async_copy(w_gate.at[0, span], wg.at[span], w_sem.at[0, p]).start()
        pltpu.make_async_copy(w_up.at[0, span], wu.at[span], w_sem.at[1, p]).start()
    for p in range(PIECES):
        span = pl.ds(p * (hidden_units // PIECES), hidden_units // PIECES)
        pltpu.make_async_copy(w_down.at[0, span], wd.at[span], w_sem.at[2, p]).start()

    def own(k):
        return pltpu.make_async_copy(
            states.at[0, 0, pl.ds(k * hc, hc)], cand[k].at[e], own_sem.at[k]
        )

    for k in range(chunks):
        own(k).start()
    for j in range(SUB):
        row[j : j + 1, :] = hid[0, :, j * width : (j + 1) * width].astype(f32)
    rows[q, z] = row[...]
    pl.semaphore_wait(barrier, 15)

    def row_copy(step):
        there = (z + step) % 4
        return remote(
            row, rows.at[q, z], row_send.at[step - 1], row_recv.at[step - 1], there * 2 + c, be
        )

    def row_arrival(step):
        come = (z - step + 4) % 4
        return remote(
            row, rows.at[q, come], row_send.at[step - 1], row_recv.at[step - 1], come * 2 + c, be
        )

    for step in range(1, 4):
        row_copy(step).start()

    def state_copy(k, slot, expert):
        return remote(
            states.at[0, 0, pl.ds(k * hc, hc)], cand[k].at[e],
            st_send.at[k, slot], st_recv.at[k, e], expert, be,
        )

    def arrival(k, index):
        return remote(
            cand[k].at[index], cand[k].at[index], st_send.at[k, 0], st_recv.at[k, index], sib, be
        )

    def forward(k, slot, index):
        return remote(
            cand[k].at[index], cand[k].at[index],
            fwd_send.at[k, slot], st_recv.at[k, index], sib, be,
        )

    def pick_copy(k):
        return remote(
            picked.at[k], cand[k].at[8], pick_send.at[k], st_recv.at[k, 8], edge, be
        )

    for k in range(chunks):
        state_copy(k, 0, far).start()

        @pl.when(outer)
        def _():
            state_copy(k, 1, near).start()

        state_copy(k, 2, sib).start()

    for step in range(1, 4):
        row_arrival(step).wait_recv()

    def block_copy(step):
        to = (q + step) % 4
        return remote(
            rows.at[q], rows.at[q], block_send.at[step - 1], block_recv.at[step - 1],
            z * 2 + to // 2, to % 2,
        )

    def block_arrival(step):
        come = (q - step + 4) % 4
        return remote(
            rows.at[come], rows.at[come], block_send.at[step - 1], block_recv.at[step - 1],
            z * 2 + come // 2, come % 2,
        )

    for step in range(1, 4):
        block_copy(step).start()
    for step in range(1, 4):
        block_arrival(step).wait_recv()

    for j in range(SUB):
        xb[j] = rows[:, :, j, :].reshape(16, width).astype(jnp.bfloat16)
    gate_acc[...] = jnp.zeros_like(gate_acc)
    up_acc[...] = jnp.zeros_like(up_acc)
    per = SUB // PIECES

    @pl.loop(0, PIECES)
    def _(p):
        span = pl.ds(pl.multiple_of(p * (depth // PIECES), depth // PIECES), depth // PIECES)
        pltpu.make_async_copy(w_gate.at[0, span], wg.at[span], w_sem.at[0, p]).wait()
        pltpu.make_async_copy(w_up.at[0, span], wu.at[span], w_sem.at[1, p]).wait()
        for i in range(per):
            j = p * per + i
            cut = pl.ds(pl.multiple_of(j * width, width), width)
            gate_acc[...] += jnp.dot(xb[j], wg[cut, :], preferred_element_type=f32)
            up_acc[...] += jnp.dot(xb[j], wu[cut, :], preferred_element_type=f32)

    for p in range(PIECES):
        span = pl.ds(p * (hidden_units // PIECES), hidden_units // PIECES)
        pltpu.make_async_copy(w_down.at[0, span], wd.at[span], w_sem.at[2, p]).wait()
    gate_val = gate_acc[...]
    middle = (gate_val / (1.0 + jnp.exp(-gate_val)) * up_acc[...]).astype(jnp.bfloat16)
    for j in range(SUB):
        value = jnp.dot(
            middle, wd[:, j * width : (j + 1) * width], preferred_element_type=f32
        )
        part[:, :, j, :] = value.reshape(4, 4, width)

    def part_copy(step):
        to = (q + step) % 4
        return remote(
            part.at[to], part_in.at[step - 1], part_send.at[step - 1], part_recv.at[step - 1],
            z * 2 + to // 2, to % 2,
        )

    for step in range(1, 4):
        part_copy(step).start()

    flat = qkv[:, 0, 0].astype(f32).reshape(3 * heads, qkv.shape[4])
    padded = jnp.concatenate([flat, jnp.zeros((128 - 3 * heads, 128), f32)], axis=0)
    columns = padded.T
    values = qkv[2, 0, 0].astype(f32)

    def out_copy(k):
        return pltpu.make_async_copy(
            fresh.at[pl.ds(k * hc, hc)], new_states.at[0, 0, pl.ds(k * hc, hc)], out_sem.at[k]
        )

    def sum_copy(step):
        there = (z + step) % 4
        return remote(
            summed.at[there], final.at[z], sum_send.at[step - 1], sum_recv.at[step - 1],
            there * 2 + c, be,
        )

    def sum_arrival(step):
        come = (z - step + 4) % 4
        return remote(
            summed.at[come], final.at[come], sum_send.at[step - 1], sum_recv.at[step - 1],
            come * 2 + c, be,
        )

    mine = parents[e, 0]
    wanted = parents[edge, 0]
    index = jnp.where(inner | (mine // 2 == z), mine, 8)

    for k in range(chunks):
        own(k).wait()

        @pl.when(inner)
        def _():
            for slot, source in enumerate((edge, far, far_edge)):
                arrival(k, source).wait_recv()
                forward(k, slot, source).start()
            arrival(k, sib).wait_recv()
            for source in (edge, far, far_edge):
                arrival(k, flip(source)).wait_recv()
            picked[k] = cand[k][wanted]
            pick_copy(k).start()

        @pl.when(outer)
        def _():
            arrival(k, sib).wait_recv()
            arrival(k, 8).wait_recv()

        for h in range(hc):
            head = k * hc + h
            parent = cand[k][index, h].astype(f32)
            key = columns[:, heads + head : heads + head + 1]
            query = columns[:, head : head + 1]
            updated = decay[0, 0, head] * parent + key * values[head : head + 1, :]
            fresh[head] = updated.astype(jnp.bfloat16)
            raw[head : head + 1, :] = jnp.sum(query * updated, axis=0, keepdims=True)
        out_copy(k).start()

        if k == 0:
            for step in range(1, 4):
                part_copy(step).wait_recv()
            summed[...] = part[q] + part_in[0] + part_in[1] + part_in[2]
            for step in range(1, 4):
                sum_copy(step).start()
            final[z] = summed[z]

    raw_out = raw[...]
    scale = lax.rsqrt(jnp.mean(raw_out * raw_out, axis=-1, keepdims=True) + 1e-05)
    readout[0, 0] = (raw_out * scale).astype(jnp.bfloat16)

    for step in range(1, 4):
        sum_arrival(step).wait_recv()
    total = jnp.zeros((SUB, width), f32)
    for x in range(4):
        weight = jnp.float32(0.0)
        for t in range(ids.shape[2]):
            weight += jnp.where(ids[0, be, t] == x, gates[0, be, t], jnp.float32(0.0))
        total += weight * final[x]
    for j in range(SUB):
        mixed[0, :, j * width : (j + 1) * width] = total[j : j + 1, :].astype(jnp.bfloat16)

    for step in range(1, 4):
        row_copy(step).wait_send()
        block_copy(step).wait_send()
        part_copy(step).wait_send()
        sum_copy(step).wait_send()
    for k in range(chunks):
        out_copy(k).wait()
        state_copy(k, 0, far).wait_send()
        state_copy(k, 2, sib).wait_send()

        @pl.when(outer)
        def _():
            state_copy(k, 1, near).wait_send()

        @pl.when(inner)
        def _():
            for slot, source in enumerate((edge, far, far_edge)):
                forward(k, slot, source).wait_send()
            pick_copy(k).wait_send()


def fused(
    states, qkv_rows, decay_rate, parents, hidden, expert_ids, gate_weights, w_gate, w_up, w_down
):
    heads, dim = states.shape[2], states.shape[3]
    depth, units = w_gate.shape[1], w_gate.shape[2]
    width = depth // SUB
    hc = heads // CHUNKS
    f32, bf16 = jnp.float32, jnp.bfloat16
    smem = pl.BlockSpec(memory_space=pltpu.SMEM)
    vmem = pl.BlockSpec(memory_space=pltpu.VMEM)
    anywhere = pl.BlockSpec(memory_space=pl.ANY)
    dma = pltpu.SemaphoreType.DMA
    scratch = [
        pltpu.VMEM((SUB, width), f32),
        pltpu.VMEM((4, 4, SUB, width), f32),
        pltpu.VMEM((SUB, 16, width), bf16),
        pltpu.VMEM((16, units), f32),
        pltpu.VMEM((16, units), f32),
        pltpu.VMEM((4, 4, SUB, width), f32),
        pltpu.VMEM((3, 4, SUB, width), f32),
        pltpu.VMEM((4, SUB, width), f32),
        pltpu.VMEM((4, SUB, width), f32),
        pltpu.VMEM((heads, dim), f32),
        pltpu.VMEM((depth, units), bf16),
        pltpu.VMEM((depth, units), bf16),
        pltpu.VMEM((units, depth), bf16),
        pltpu.VMEM((CHUNKS, hc, dim, dim), bf16),
        pltpu.VMEM((heads, dim, dim), bf16),
        dma((3,)), dma((3,)), dma((3,)), dma((3,)), dma((3,)), dma((3,)), dma((3,)), dma((3,)),
        dma((3, PIECES)), dma((CHUNKS,)), dma((CHUNKS,)),
        dma((CHUNKS, 3)), dma((CHUNKS, 9)), dma((CHUNKS, 3)), dma((CHUNKS,)),
    ] + [pltpu.VMEM((9, hc, dim, dim), bf16) for _ in range(CHUNKS)]
    return pl.pallas_call(
        fused_kernel,
        out_shape=(
            jax.ShapeDtypeStruct(states.shape, bf16),
            jax.ShapeDtypeStruct(qkv_rows.shape[1:], bf16),
            jax.ShapeDtypeStruct(hidden.shape, bf16),
        ),
        in_specs=[smem] * 4 + [vmem] * 2 + [anywhere] * 4,
        out_specs=(anywhere, vmem, vmem),
        scratch_shapes=scratch,
        compiler_params=pltpu.CompilerParams(
            collective_id=0, has_side_effects=True, vmem_limit_bytes=50 * 1024 * 1024
        ),
        cost_estimate=pl.CostEstimate(
            flops=6 * 16 * depth * units, bytes_accessed=6 * depth * units, transcendentals=0
        ),
    )(
        parents, decay_rate, expert_ids, gate_weights, qkv_rows, hidden, states,
        w_gate, w_up, w_down,
    )


def solution(mesh):
    in_specs = (
        P("expert", ("groups", "beam"), "head", None, None),
        P(None, "expert", ("groups", "beam"), "head", None),
        P("expert", ("groups", "beam"), "head"),
        P(None, ("groups", "beam")),
        P("expert", ("groups", "beam"), None),
        P("expert", "groups", None),
        P("expert", "groups", None),
        P("expert", None, ("beam", "head")),
        P("expert", None, ("beam", "head")),
        P("expert", ("beam", "head"), None),
    )
    out_specs = (
        P("expert", ("groups", "beam"), "head", None, None),
        P("expert", ("groups", "beam"), "head", None),
        P("expert", ("groups", "beam"), "head"),
    )
    sizes = mesh.shape
    fits = sizes["expert"] == 8 and sizes["beam"] == 2 and sizes["head"] == 1
    body = fused if fits else local
    return jax.shard_map(body, mesh=mesh, in_specs=in_specs, out_specs=out_specs, check_vma=False)
```

```python
import functools
import jax
import jax.numpy as jnp
from jax import lax
from jax.experimental import pallas as pl
from jax.experimental.pallas import tpu as pltpu
from jax.sharding import PartitionSpec as P


def local(
    states, qkv_rows, decay_rate, parents, hidden, expert_ids, gate_weights, w_gate, w_up, w_down
):
    beam_index = lax.axis_index("expert")
    parent_ids = lax.dynamic_index_in_dim(parents, beam_index, 0, keepdims=False)
    shard_piece = lax.all_gather(states, "expert", axis=0, tiled=True)
    source_ids = jnp.arange(shard_piece.shape[0], dtype=jnp.int32)
    matches = source_ids[:, None] == parent_ids[None, :]
    chosen = jnp.sum(
        jnp.where(matches[:, :, None, None, None], shard_piece, jnp.zeros((), jnp.bfloat16)), axis=0
    )
    query = qkv_rows[0, 0].astype(jnp.float32)
    key_part = qkv_rows[1, 0].astype(jnp.float32)
    value_part = qkv_rows[2, 0].astype(jnp.float32)
    updated = (
        decay_rate[0][..., None, None] * chosen.astype(jnp.float32)
        + key_part[..., :, None] * value_part[..., None, :]
    )
    new_states = updated.astype(jnp.bfloat16)[None]
    raw_out = jnp.einsum("rhk,rhkv->rhv", query, updated, precision=lax.Precision.HIGHEST)
    readout = (
        raw_out * lax.rsqrt(jnp.mean(raw_out * raw_out, axis=-1, keepdims=True) + 1e-05)
    ).astype(jnp.bfloat16)[None]
    beam_block = lax.all_gather(hidden, "beam", axis=1, tiled=True)[0]
    route_ids = expert_ids[0]
    route_gates = gate_weights[0]
    request_count = beam_block.shape[0]
    top_count = route_ids.shape[1]
    expert_count = lax.axis_size("expert") // 2
    capacity = min(request_count, 2 * request_count * top_count // expert_count)
    expert_range = jnp.arange(expert_count, dtype=jnp.int32)
    flat_ids = route_ids.reshape(-1)
    one_hot = (flat_ids[None, :] == expert_range[:, None]).astype(jnp.int32)
    slot_rank = jnp.cumsum(one_hot, axis=1) - 1
    slot_range = jnp.arange(capacity, dtype=jnp.int32)
    assignment = one_hot[:, :, None] * (slot_rank[:, :, None] == slot_range[None, None, :]).astype(
        jnp.int32
    )
    placement = assignment.reshape(expert_count, request_count, top_count, capacity).sum(axis=2)
    gate_select = jnp.sum(
        jnp.where(
            route_ids[None, :, :] == expert_range[:, None, None],
            route_gates[None, :, :],
            jnp.zeros((), jnp.float32),
        ),
        axis=2,
    )
    combine_weight = placement.astype(jnp.float32) * gate_select[:, :, None]
    dispatched = jnp.einsum(
        "xrc,rd->xcd",
        placement.astype(jnp.bfloat16),
        beam_block,
        preferred_element_type=jnp.float32,
    ).astype(jnp.bfloat16)
    outgoing = jnp.repeat(dispatched, 2, axis=0)
    arrived = lax.all_to_all(outgoing, "expert", split_axis=0, concat_axis=0, tiled=True)
    gate_val = jnp.einsum("scd,df->scf", arrived, w_gate[0], preferred_element_type=jnp.float32)
    up_val = jnp.einsum("scd,df->scf", arrived, w_up[0], preferred_element_type=jnp.float32)
    middle = (jax.nn.silu(gate_val) * up_val).astype(jnp.bfloat16)
    partial_value = jnp.einsum("scf,fd->scd", middle, w_down[0], preferred_element_type=jnp.float32)
    returned = lax.all_to_all(partial_value, "expert", split_axis=0, concat_axis=0, tiled=True)
    paired = returned.reshape(expert_count, 2, capacity, returned.shape[2]).sum(axis=1)
    partial_rows = jnp.einsum(
        "xrc,xcd->rd", combine_weight, paired, precision=lax.Precision.HIGHEST
    )
    beam_size = lax.axis_size("beam")
    head_size = lax.axis_size("head")
    local_rows = request_count // beam_size
    model_width = partial_rows.shape[1]
    arranged = partial_rows.reshape(beam_size, local_rows, head_size, model_width // head_size)
    arranged = arranged.transpose(0, 2, 1, 3).reshape(
        beam_size * head_size * local_rows, model_width // head_size
    )
    summed = lax.psum_scatter(arranged, ("beam", "head"), scatter_dimension=0, tiled=True)
    mixed = summed.astype(jnp.bfloat16).reshape(1, local_rows, model_width // head_size)
    return (new_states, readout, mixed)


CHUNKS = 8
PIECES = 4
SUB = 8


def fused_kernel(
    parents, decay, ids, gates, qkv, hid, states, w_gate, w_up, w_down,
    new_states, readout, mixed,
    row, rows, xb, gate_acc, up_acc, part, part_in, summed, final, raw,
    wg, wu, wd, picked, fresh,
    row_send, row_recv, block_send, block_recv, part_send, part_recv, sum_send, sum_recv,
    w_sem, own_sem, out_sem, st_send, st_recv, fwd_send, pick_send,
    *cand,
):
    e = lax.axis_index("expert")
    be = lax.axis_index("beam")
    z, c = e // 2, e % 2
    q = c * 2 + be
    side = z // 2
    inner = (z == 1) | (z == 2)
    outer = (z == 0) | (z == 3)
    sib = z * 2 + (1 - c)
    near = (1 + side) * 2 + c
    far = (2 - side) * 2 + c
    edge = 3 * side * 2 + c
    far_edge = 3 * (1 - side) * 2 + c
    chunks = len(cand)
    heads = qkv.shape[3]
    hc = heads // chunks
    width = row.shape[1]
    depth, hidden_units = w_gate.shape[1], w_gate.shape[2]
    f32 = jnp.float32

    def flip(index):
        return index + 1 - 2 * c

    def remote(src, dst, ssem, rsem, expert, beam):
        return pltpu.make_async_remote_copy(
            src_ref=src, dst_ref=dst, send_sem=ssem, recv_sem=rsem,
            device_id={"expert": expert, "beam": beam}, device_id_type=pl.DeviceIdType.MESH,
        )

    barrier = pltpu.get_barrier_semaphore()
    for step in range(1, 16):
        other = (e * 2 + be + step) % 16
        pl.semaphore_signal(
            barrier, inc=1, device_id={"expert": other // 2, "beam": other % 2},
            device_id_type=pl.DeviceIdType.MESH,
        )

    for p in range(PIECES):
        span = pl.ds(p * (depth // PIECES), depth // PIECES)
        pltpu.make_async_copy(w_gate.at[0, span], wg.at[span], w_sem.at[0, p]).start()
        pltpu.make_async_copy(w_up.at[0, span], wu.at[span], w_sem.at[1, p]).start()
    for p in range(PIECES):
        span = pl.ds(p * (hidden_units // PIECES), hidden_units // PIECES)
        pltpu.make_async_copy(w_down.at[0, span], wd.at[span], w_sem.at[2, p]).start()

    def own(k):
        return pltpu.make_async_copy(
            states.at[0, 0, pl.ds(k * hc, hc)], cand[k].at[e], own_sem.at[k]
        )

    for k in range(chunks):
        own(k).start()
    for j in range(SUB):
        row[j : j + 1, :] = hid[0, :, j * width : (j + 1) * width].astype(f32)
    rows[q, z] = row[...]
    pl.semaphore_wait(barrier, 15)

    def row_copy(step):
        there = (z + step) % 4
        return remote(
            row, rows.at[q, z], row_send.at[step - 1], row_recv.at[step - 1], there * 2 + c, be
        )

    def row_arrival(step):
        come = (z - step + 4) % 4
        return remote(
            row, rows.at[q, come], row_send.at[step - 1], row_recv.at[step - 1], come * 2 + c, be
        )

    for step in range(1, 4):
        row_copy(step).start()

    def state_copy(k, slot, expert):
        return remote(
            states.at[0, 0, pl.ds(k * hc, hc)], cand[k].at[e],
            st_send.at[k, slot], st_recv.at[k, e], expert, be,
        )

    def arrival(k, index):
        return remote(
            cand[k].at[index], cand[k].at[index], st_send.at[k, 0], st_recv.at[k, index], sib, be
        )

    def forward(k, slot, index):
        return remote(
            cand[k].at[index], cand[k].at[index],
            fwd_send.at[k, slot], st_recv.at[k, index], sib, be,
        )

    def pick_copy(k):
        return remote(
            picked.at[k], cand[k].at[8], pick_send.at[k], st_recv.at[k, 8], edge, be
        )

    for k in range(chunks):
        state_copy(k, 0, far).start()

        @pl.when(outer)
        def _():
            state_copy(k, 1, near).start()

        state_copy(k, 2, sib).start()

    for step in range(1, 4):
        row_arrival(step).wait_recv()

    def block_copy(step):
        to = (q + step) % 4
        return remote(
            rows.at[q], rows.at[q], block_send.at[step - 1], block_recv.at[step - 1],
            z * 2 + to // 2, to % 2,
        )

    def block_arrival(step):
        come = (q - step + 4) % 4
        return remote(
            rows.at[come], rows.at[come], block_send.at[step - 1], block_recv.at[step - 1],
            z * 2 + come // 2, come % 2,
        )

    for step in range(1, 4):
        block_copy(step).start()
    for step in range(1, 4):
        block_arrival(step).wait_recv()

    for j in range(SUB):
        xb[j] = rows[:, :, j, :].reshape(16, width).astype(jnp.bfloat16)
    gate_acc[...] = jnp.zeros_like(gate_acc)
    up_acc[...] = jnp.zeros_like(up_acc)
    per = SUB // PIECES

    @pl.loop(0, PIECES)
    def _(p):
        span = pl.ds(pl.multiple_of(p * (depth // PIECES), depth // PIECES), depth // PIECES)
        pltpu.make_async_copy(w_gate.at[0, span], wg.at[span], w_sem.at[0, p]).wait()
        pltpu.make_async_copy(w_up.at[0, span], wu.at[span], w_sem.at[1, p]).wait()
        for i in range(per):
            j = p * per + i
            cut = pl.ds(pl.multiple_of(j * width, width), width)
            gate_acc[...] += jnp.dot(xb[j], wg[cut, :], preferred_element_type=f32)
            up_acc[...] += jnp.dot(xb[j], wu[cut, :], preferred_element_type=f32)

    for p in range(PIECES):
        span = pl.ds(p * (hidden_units // PIECES), hidden_units // PIECES)
        pltpu.make_async_copy(w_down.at[0, span], wd.at[span], w_sem.at[2, p]).wait()
    gate_val = gate_acc[...]
    middle = (gate_val / (1.0 + jnp.exp(-gate_val)) * up_acc[...]).astype(jnp.bfloat16)
    for j in range(SUB):
        value = jnp.dot(
            middle, wd[:, j * width : (j + 1) * width], preferred_element_type=f32
        )
        part[:, :, j, :] = value.reshape(4, 4, width)

    def part_copy(step):
        to = (q + step) % 4
        return remote(
            part.at[to], part_in.at[step - 1], part_send.at[step - 1], part_recv.at[step - 1],
            z * 2 + to // 2, to % 2,
        )

    for step in range(1, 4):
        part_copy(step).start()

    flat = qkv[:, 0, 0].astype(f32).reshape(3 * heads, qkv.shape[4])
    padded = jnp.concatenate([flat, jnp.zeros((128 - 3 * heads, 128), f32)], axis=0)
    columns = padded.T
    values = qkv[2, 0, 0].astype(f32)

    def out_copy(k):
        return pltpu.make_async_copy(
            fresh.at[pl.ds(k * hc, hc)], new_states.at[0, 0, pl.ds(k * hc, hc)], out_sem.at[k]
        )

    def sum_copy(step):
        there = (z + step) % 4
        return remote(
            summed.at[there], final.at[z], sum_send.at[step - 1], sum_recv.at[step - 1],
            there * 2 + c, be,
        )

    def sum_arrival(step):
        come = (z - step + 4) % 4
        return remote(
            summed.at[come], final.at[come], sum_send.at[step - 1], sum_recv.at[step - 1],
            come * 2 + c, be,
        )

    mine = parents[e, 0]
    wanted = parents[edge, 0]
    index = jnp.where(inner | (mine // 2 == z), mine, 8)

    for k in range(chunks):
        own(k).wait()

        @pl.when(inner)
        def _():
            for slot, source in enumerate((edge, far, far_edge)):
                arrival(k, source).wait_recv()
                forward(k, slot, source).start()
            arrival(k, sib).wait_recv()
            for source in (edge, far, far_edge):
                arrival(k, flip(source)).wait_recv()
            picked[k] = cand[k][wanted]
            pick_copy(k).start()

        @pl.when(outer)
        def _():
            arrival(k, sib).wait_recv()
            arrival(k, 8).wait_recv()

        for h in range(hc):
            head = k * hc + h
            parent = cand[k][index, h].astype(f32)
            key = columns[:, heads + head : heads + head + 1]
            query = columns[:, head : head + 1]
            updated = decay[0, 0, head] * parent + key * values[head : head + 1, :]
            fresh[head] = updated.astype(jnp.bfloat16)
            raw[head : head + 1, :] = jnp.sum(query * updated, axis=0, keepdims=True)
        out_copy(k).start()

        if k == 0:
            for step in range(1, 4):
                part_copy(step).wait_recv()
            summed[...] = part[q] + part_in[0] + part_in[1] + part_in[2]
            for step in range(1, 4):
                sum_copy(step).start()
            final[z] = summed[z]

    raw_out = raw[...]
    scale = lax.rsqrt(jnp.mean(raw_out * raw_out, axis=-1, keepdims=True) + 1e-05)
    readout[0, 0] = (raw_out * scale).astype(jnp.bfloat16)

    for step in range(1, 4):
        sum_arrival(step).wait_recv()
    total = jnp.zeros((SUB, width), f32)
    for x in range(4):
        weight = jnp.float32(0.0)
        for t in range(ids.shape[2]):
            weight += jnp.where(ids[0, be, t] == x, gates[0, be, t], jnp.float32(0.0))
        total += weight * final[x]
    for j in range(SUB):
        mixed[0, :, j * width : (j + 1) * width] = total[j : j + 1, :].astype(jnp.bfloat16)

    for step in range(1, 4):
        row_copy(step).wait_send()
        block_copy(step).wait_send()
        part_copy(step).wait_send()
        sum_copy(step).wait_send()
    for k in range(chunks):
        out_copy(k).wait()
        state_copy(k, 0, far).wait_send()
        state_copy(k, 2, sib).wait_send()

        @pl.when(outer)
        def _():
            state_copy(k, 1, near).wait_send()

        @pl.when(inner)
        def _():
            for slot, source in enumerate((edge, far, far_edge)):
                forward(k, slot, source).wait_send()
            pick_copy(k).wait_send()


def fused(
    states, qkv_rows, decay_rate, parents, hidden, expert_ids, gate_weights, w_gate, w_up, w_down
):
    heads, dim = states.shape[2], states.shape[3]
    depth, units = w_gate.shape[1], w_gate.shape[2]
    width = depth // SUB
    hc = heads // CHUNKS
    f32, bf16 = jnp.float32, jnp.bfloat16
    smem = pl.BlockSpec(memory_space=pltpu.SMEM)
    vmem = pl.BlockSpec(memory_space=pltpu.VMEM)
    anywhere = pl.BlockSpec(memory_space=pl.ANY)
    dma = pltpu.SemaphoreType.DMA
    scratch = [
        pltpu.VMEM((SUB, width), f32),
        pltpu.VMEM((4, 4, SUB, width), f32),
        pltpu.VMEM((SUB, 16, width), bf16),
        pltpu.VMEM((16, units), f32),
        pltpu.VMEM((16, units), f32),
        pltpu.VMEM((4, 4, SUB, width), f32),
        pltpu.VMEM((3, 4, SUB, width), f32),
        pltpu.VMEM((4, SUB, width), f32),
        pltpu.VMEM((4, SUB, width), f32),
        pltpu.VMEM((heads, dim), f32),
        pltpu.VMEM((depth, units), bf16),
        pltpu.VMEM((depth, units), bf16),
        pltpu.VMEM((units, depth), bf16),
        pltpu.VMEM((CHUNKS, hc, dim, dim), bf16),
        pltpu.VMEM((heads, dim, dim), bf16),
        dma((3,)), dma((3,)), dma((3,)), dma((3,)), dma((3,)), dma((3,)), dma((3,)), dma((3,)),
        dma((3, PIECES)), dma((CHUNKS,)), dma((CHUNKS,)),
        dma((CHUNKS, 3)), dma((CHUNKS, 9)), dma((CHUNKS, 3)), dma((CHUNKS,)),
    ] + [pltpu.VMEM((9, hc, dim, dim), bf16) for _ in range(CHUNKS)]
    return pl.pallas_call(
        fused_kernel,
        out_shape=(
            jax.ShapeDtypeStruct(states.shape, bf16),
            jax.ShapeDtypeStruct(qkv_rows.shape[1:], bf16),
            jax.ShapeDtypeStruct(hidden.shape, bf16),
        ),
        in_specs=[smem] * 4 + [vmem] * 2 + [anywhere] * 4,
        out_specs=(anywhere, vmem, vmem),
        scratch_shapes=scratch,
        compiler_params=pltpu.CompilerParams(
            collective_id=0, has_side_effects=True, vmem_limit_bytes=50 * 1024 * 1024
        ),
        cost_estimate=pl.CostEstimate(
            flops=6 * 16 * depth * units, bytes_accessed=6 * depth * units, transcendentals=0
        ),
    )(
        parents, decay_rate, expert_ids, gate_weights, qkv_rows, hidden, states,
        w_gate, w_up, w_down,
    )


SLOTS = 3
STEPS = 16


def routed_kernel(
    parents_in, decay_in, ids_in, gates_in, qkv_in, hid_in, states, w_gate, w_up, w_down,
    new_states, readout, mixed, flag,
    row, rows, xb, gate_acc, up_acc, middle, part, part_in, summed, final, raw,
    wg, wu, wd, picked, extra, edged, fresh, mark, marks,
    parents, decay, ids, gates, qkv, hid,
    small_sem, mark_send, mark_recv,
    row_send, row_recv, block_send, block_recv, part_send, part_recv, sum_send, sum_recv,
    w_sem, own_sem, out_sem, st_send, a_recv, b_recv, fwd_send, pick_send,
    *cand,
):
    steps = len(cand) // 2
    near_set, far_set = cand[:steps], cand[steps:]
    g = lax.axis_index("groups")
    e = lax.axis_index("expert")
    be = lax.axis_index("beam")
    z, c = e // 2, e % 2
    q = c * 2 + be
    side = z // 2
    inner = (z == 1) | (z == 2)
    outer = (z == 0) | (z == 3)
    sib = z * 2 + (1 - c)
    near = (1 + side) * 2 + c
    far = (2 - side) * 2 + c
    edge = 3 * side * 2 + c
    heads = qkv.shape[3]
    hc = heads // steps
    width = row.shape[1]
    depth, hidden_units = w_gate.shape[1], w_gate.shape[2]
    f32 = jnp.float32

    def remote(src, dst, ssem, rsem, expert, beam):
        return pltpu.make_async_remote_copy(
            src_ref=src, dst_ref=dst, send_sem=ssem, recv_sem=rsem,
            device_id={"expert": expert, "beam": beam}, device_id_type=pl.DeviceIdType.MESH,
        )

    small = [
        pltpu.make_async_copy(src, dst, small_sem.at[i])
        for i, (src, dst) in enumerate(
            (
                (hid_in, hid), (parents_in, parents), (qkv_in, qkv),
                (decay_in, decay), (ids_in, ids), (gates_in, gates),
            )
        )
    ]
    for copy in small:
        copy.start()

    barrier = pltpu.get_barrier_semaphore()
    for step in range(1, 16):
        other = (e * 2 + be + step) % 16
        pl.semaphore_signal(
            barrier, inc=1, device_id={"expert": other // 2, "beam": other % 2},
            device_id_type=pl.DeviceIdType.MESH,
        )
    for beam in range(2):
        pl.semaphore_signal(
            barrier, inc=1, device_id={"groups": 1 - g, "beam": beam},
            device_id_type=pl.DeviceIdType.MESH,
        )

    def own(k):
        return pltpu.make_async_copy(
            states.at[0, 0, pl.ds(k * hc, hc)], near_set[k].at[c], own_sem.at[k]
        )

    small[0].wait()
    for j in range(SUB):
        row[j : j + 1, :] = hid[0, :, j * width : (j + 1) * width].astype(f32)
    rows[q, z] = row[...]

    small[1].wait()
    zero, one = jnp.int32(0), jnp.int32(1)

    def needed(base, takers):
        found = []
        for j in range(4):
            hit = zero
            for i in range(4):
                hit = jnp.where(parents[0, takers + i] == base + j, one, hit)
            found.append(hit)
        return found

    my_base, other_base = 4 * side, 4 * (1 - side)
    going = needed(my_base, other_base)
    coming = needed(other_base, my_base)

    def rank_of(found, j):
        total = zero
        for i in range(4):
            total += jnp.where(i < j, found[i], zero)
        return jnp.minimum(total, SLOTS - 1)

    def entry_of(j):
        return (j & 1) + jnp.where(((j >> 1) & 1) == 1 - side, 0, 2)

    def chosen(slot):
        pick, before = zero, zero
        for j in range(4):
            pick = jnp.where((going[j] == 1) & (before == slot), jnp.int32(j), pick)
            before += going[j]
        return entry_of(pick)

    slot_entry = [chosen(slot) for slot in range(SLOTS)]
    my_slot = jnp.where(c == 0, slot_entry[0], slot_entry[1])
    overflow = (sum(going) > SLOTS) | (sum(coming) > SLOTS)
    mark[...] = jnp.zeros_like(mark) + jnp.where(overflow, f32(1.0), f32(0.0))

    wanted = parents[0, edge]
    edge_far = (wanted >> 2) != side
    edge_near_entry = entry_of(wanted & 3)
    edge_slot = rank_of(coming, wanted & 3)
    mine = parents[0, e]
    chip_own = (mine >> 1) == z
    use_far = jnp.where(inner, jnp.where((mine >> 2) != side, one, zero), jnp.where(chip_own, zero, one)) == 1
    near_entry = jnp.where(inner, entry_of(mine & 3), mine & 1)
    far_entry = jnp.where(inner, rank_of(coming, mine & 3), zero)

    pl.semaphore_wait(barrier, 17)

    def row_copy(step):
        there = (z + step) % 4
        return remote(
            row, rows.at[q, z], row_send.at[step - 1], row_recv.at[step - 1], there * 2 + c, be
        )

    def row_arrival(step):
        come = (z - step + 4) % 4
        return remote(
            row, rows.at[q, come], row_send.at[step - 1], row_recv.at[step - 1], come * 2 + c, be
        )

    def state_copy(k, slot, expert, entry):
        return remote(
            states.at[0, 0, pl.ds(k * hc, hc)], near_set[k].at[entry],
            st_send.at[k, slot], a_recv.at[k, entry], expert, be,
        )

    def near_arrival(k, entry):
        there = near_set[k].at[entry]
        return remote(there, there, st_send.at[k, 0], a_recv.at[k, entry], sib, be)

    def far_arrival(k, entry):
        there = far_set[k].at[entry]
        return remote(there, there, st_send.at[k, 0], b_recv.at[k, entry], sib, be)

    def near_forward(k):
        there = near_set[k].at[2 + c]
        return remote(there, there, fwd_send.at[k, 0], a_recv.at[k, 2 + c], sib, be)

    def far_forward(k, slot, entry):
        there = far_set[k].at[entry]
        return remote(there, there, fwd_send.at[k, slot], b_recv.at[k, entry], sib, be)

    def slot_copy(k):
        return remote(
            picked.at[k], far_set[k].at[c], pick_send.at[k, 0], b_recv.at[k, c], far, be
        )

    def extra_copy(k):
        return remote(
            extra.at[k // 2], far_set[k].at[2], pick_send.at[k, 1], b_recv.at[k, 2], far, be
        )

    def edge_copy(k):
        return remote(
            edged.at[k], far_set[k].at[0], pick_send.at[k, 2], b_recv.at[k, 0], edge, be
        )

    for k in range(steps):
        @pl.when(outer)
        def _():
            state_copy(k, 1, near, 2 + c).start()

        state_copy(k, 0, sib, c).start()
        own(k).start()
        if k == 0:
            for step in range(1, 4):
                row_copy(step).start()

    def mark_copy(step):
        column = (g * 2 + be + step) % 4
        return pltpu.make_async_remote_copy(
            src_ref=mark, dst_ref=marks.at[step - 1], send_sem=mark_send.at[step - 1],
            recv_sem=mark_recv.at[step - 1],
            device_id={"groups": column // 2, "beam": column % 2},
            device_id_type=pl.DeviceIdType.MESH,
        )

    for step in range(1, 4):
        mark_copy(step).start()

    for p in range(PIECES):
        span = pl.ds(p * (depth // PIECES), depth // PIECES)
        pltpu.make_async_copy(w_gate.at[0, span], wg.at[span], w_sem.at[0, p]).start()
        pltpu.make_async_copy(w_up.at[0, span], wu.at[span], w_sem.at[1, p]).start()
    for p in range(PIECES):
        span = pl.ds(p * (hidden_units // PIECES), hidden_units // PIECES)
        pltpu.make_async_copy(w_down.at[0, span], wd.at[span], w_sem.at[2, p]).start()

    def pass_near(k):
        @pl.when(inner)
        def _():
            near_arrival(k, 2 + c).wait_recv()
            near_forward(k).start()

    def send_slots(k):
        own(k).wait()
        near_arrival(k, 1 - c).wait_recv()

        @pl.when(inner)
        def _():
            near_arrival(k, 3 - c).wait_recv()
            picked[k] = near_set[k][my_slot]
            slot_copy(k).start()

        @pl.when(inner & (c == k % 2))
        def _():
            extra[k // 2] = near_set[k][slot_entry[2]]
            extra_copy(k).start()

    def pass_far(k):
        @pl.when(inner)
        def _():
            far_arrival(k, c).wait_recv()
            far_forward(k, 1, c).start()

        @pl.when(inner & (c == k % 2))
        def _():
            far_arrival(k, 2).wait_recv()
            far_forward(k, 2, 2).start()

    def out_copy(k):
        return pltpu.make_async_copy(
            fresh.at[pl.ds(k * hc, hc)], new_states.at[0, 0, pl.ds(k * hc, hc)], out_sem.at[k]
        )

    def send_edge(k):
        @pl.when(inner)
        def _():
            far_arrival(k, 1 - c).wait_recv()

        @pl.when(inner & (c != k % 2))
        def _():
            far_arrival(k, 2).wait_recv()

        @pl.when(inner)
        def _():
            edged[k] = jnp.where(edge_far, far_set[k][edge_slot], near_set[k][edge_near_entry])
            edge_copy(k).start()

    def finish(k):
        @pl.when(outer)
        def _():
            far_arrival(k, 0).wait_recv()

        for h in range(hc):
            head = k * hc + h
            parent = jnp.where(
                use_far, far_set[k][far_entry, h], near_set[k][near_entry, h]
            ).astype(f32)
            key = columns[:, heads + head : heads + head + 1]
            query = columns[:, head : head + 1]
            updated = decay[0, 0, head] * parent + key * values[head : head + 1, :]
            fresh[head] = updated.astype(jnp.bfloat16)
            raw[head : head + 1, :] = jnp.sum(query * updated, axis=0, keepdims=True)
        out_copy(k).start()

    def block_copy(step):
        to = (q + step) % 4
        return remote(
            rows.at[q], rows.at[q], block_send.at[step - 1], block_recv.at[step - 1],
            z * 2 + to // 2, to % 2,
        )

    def block_arrival(step):
        come = (q - step + 4) % 4
        return remote(
            rows.at[come], rows.at[come], block_send.at[step - 1], block_recv.at[step - 1],
            z * 2 + come // 2, come % 2,
        )

    def gather_first():
        for step in range(1, 4):
            row_arrival(step).wait_recv()
        for step in range(1, 4):
            block_copy(step).start()

    def gather_second():
        for step in range(1, 4):
            block_arrival(step).wait_recv()
        for j in range(SUB):
            xb[j] = rows[:, :, j, :].reshape(16, width).astype(jnp.bfloat16)
        gate_acc[...] = jnp.zeros_like(gate_acc)
        up_acc[...] = jnp.zeros_like(up_acc)

    per = SUB // PIECES

    def first_dots(p):
        span = pl.ds(p * (depth // PIECES), depth // PIECES)
        pltpu.make_async_copy(w_gate.at[0, span], wg.at[span], w_sem.at[0, p]).wait()
        pltpu.make_async_copy(w_up.at[0, span], wu.at[span], w_sem.at[1, p]).wait()
        for i in range(per):
            j = p * per + i
            cut = pl.ds(j * width, width)
            gate_acc[...] += jnp.dot(xb[j], wg[cut, :], preferred_element_type=f32)
            up_acc[...] += jnp.dot(xb[j], wu[cut, :], preferred_element_type=f32)

    def activate():
        for p in range(PIECES):
            span = pl.ds(p * (hidden_units // PIECES), hidden_units // PIECES)
            pltpu.make_async_copy(w_down.at[0, span], wd.at[span], w_sem.at[2, p]).wait()
        gate_val = gate_acc[...]
        middle[...] = (gate_val / (1.0 + jnp.exp(-gate_val)) * up_acc[...]).astype(jnp.bfloat16)

    def second_dots(p):
        for i in range(per):
            j = p * per + i
            value = jnp.dot(
                middle[...], wd[:, j * width : (j + 1) * width], preferred_element_type=f32
            )
            part[:, :, j, :] = value.reshape(4, 4, width)

    def part_copy(step):
        to = (q + step) % 4
        return remote(
            part.at[to], part_in.at[step - 1], part_send.at[step - 1], part_recv.at[step - 1],
            z * 2 + to // 2, to % 2,
        )

    def sum_copy(step):
        there = (z + step) % 4
        return remote(
            summed.at[there], final.at[z], sum_send.at[step - 1], sum_recv.at[step - 1],
            there * 2 + c, be,
        )

    def sum_arrival(step):
        come = (z - step + 4) % 4
        return remote(
            summed.at[come], final.at[come], sum_send.at[step - 1], sum_recv.at[step - 1],
            come * 2 + c, be,
        )

    def send_parts():
        for step in range(1, 4):
            part_copy(step).start()

    def send_sums():
        for step in range(1, 4):
            part_copy(step).wait_recv()
        summed[...] = part[q] + part_in[0] + part_in[1] + part_in[2]
        for step in range(1, 4):
            sum_copy(step).start()
        final[z] = summed[z]

    pass_near(0)
    for copy in small[2:]:
        copy.wait()
    flat = qkv[:, 0, 0].astype(f32).reshape(3 * heads, qkv.shape[4])
    padded = jnp.concatenate([flat, jnp.zeros((128 - 3 * heads, 128), f32)], axis=0)
    columns = padded.T
    values = qkv[2, 0, 0].astype(f32)

    work = [gather_first, gather_second]
    work += [functools.partial(first_dots, p) for p in range(PIECES)]
    work += [activate]
    work += [functools.partial(second_dots, p) for p in range(PIECES)]
    work += [send_parts]
    share = -(-len(work) // steps)
    lag, last = 3, 4
    for i in range(steps + last):
        if i < steps:
            send_slots(i)
        if i + 1 < steps:
            pass_near(i + 1)
        if 0 <= i - lag < steps:
            pass_far(i - lag)
        for unit in work[i * share : (i + 1) * share]:
            unit()
        if 0 <= i - last < steps:
            send_edge(i - last)
            finish(i - last)
        if i == steps:
            send_sums()

    raw_out = raw[...]
    scale = lax.rsqrt(jnp.mean(raw_out * raw_out, axis=-1, keepdims=True) + 1e-05)
    readout[0, 0] = (raw_out * scale).astype(jnp.bfloat16)

    for step in range(1, 4):
        sum_arrival(step).wait_recv()
    total = jnp.zeros((SUB, width), f32)
    for x in range(4):
        weight = jnp.float32(0.0)
        for t in range(ids.shape[2]):
            weight += jnp.where(ids[0, be, t] == x, gates[0, be, t], jnp.float32(0.0))
        total += weight * final[x]
    for j in range(SUB):
        mixed[0, :, j * width : (j + 1) * width] = total[j : j + 1, :].astype(jnp.bfloat16)

    for step in range(1, 4):
        mark_copy(step).wait_recv()
    flag[...] = mark[...] + marks[0] + marks[1] + marks[2]

    for step in range(1, 4):
        mark_copy(step).wait_send()
        row_copy(step).wait_send()
        block_copy(step).wait_send()
        part_copy(step).wait_send()
        sum_copy(step).wait_send()
    for k in range(steps):
        out_copy(k).wait()
        state_copy(k, 0, sib, c).wait_send()

        @pl.when(outer)
        def _():
            state_copy(k, 1, near, 2 + c).wait_send()

        @pl.when(inner)
        def _():
            near_forward(k).wait_send()
            slot_copy(k).wait_send()
            far_forward(k, 1, c).wait_send()
            edge_copy(k).wait_send()

        @pl.when(inner & (c == k % 2))
        def _():
            extra_copy(k).wait_send()
            far_forward(k, 2, 2).wait_send()


def routed(
    states, qkv_rows, decay_rate, parents, hidden, expert_ids, gate_weights, w_gate, w_up, w_down
):
    heads, dim = states.shape[2], states.shape[3]
    depth, units = w_gate.shape[1], w_gate.shape[2]
    width = depth // SUB
    hc = heads // STEPS
    f32, bf16, i32 = jnp.float32, jnp.bfloat16, jnp.int32
    vmem = pl.BlockSpec(memory_space=pltpu.VMEM)
    hbm = pl.BlockSpec(memory_space=pltpu.HBM)
    dma = pltpu.SemaphoreType.DMA
    scratch = [
        pltpu.VMEM((SUB, width), f32),
        pltpu.VMEM((4, 4, SUB, width), f32),
        pltpu.VMEM((SUB, 16, width), bf16),
        pltpu.VMEM((16, units), f32),
        pltpu.VMEM((16, units), f32),
        pltpu.VMEM((16, units), bf16),
        pltpu.VMEM((4, 4, SUB, width), f32),
        pltpu.VMEM((3, 4, SUB, width), f32),
        pltpu.VMEM((4, SUB, width), f32),
        pltpu.VMEM((4, SUB, width), f32),
        pltpu.VMEM((heads, dim), f32),
        pltpu.VMEM((depth, units), bf16),
        pltpu.VMEM((depth, units), bf16),
        pltpu.VMEM((units, depth), bf16),
        pltpu.VMEM((STEPS, hc, dim, dim), bf16),
        pltpu.VMEM(((STEPS + 1) // 2, hc, dim, dim), bf16),
        pltpu.VMEM((STEPS, hc, dim, dim), bf16),
        pltpu.VMEM((heads, dim, dim), bf16),
        pltpu.VMEM((8, 128), f32),
        pltpu.VMEM((3, 8, 128), f32),
        pltpu.SMEM((1, parents.shape[0]), i32),
        pltpu.SMEM(decay_rate.shape, f32),
        pltpu.SMEM(expert_ids.shape, i32),
        pltpu.SMEM(gate_weights.shape, f32),
        pltpu.VMEM(qkv_rows.shape, bf16),
        pltpu.VMEM(hidden.shape, bf16),
        dma((6,)), dma((3,)), dma((3,)),
        dma((3,)), dma((3,)), dma((3,)), dma((3,)), dma((3,)), dma((3,)), dma((3,)), dma((3,)),
        dma((3, PIECES)), dma((STEPS,)), dma((STEPS,)),
        dma((STEPS, 2)), dma((STEPS, 4)), dma((STEPS, 3)), dma((STEPS, 3)), dma((STEPS, 3)),
    ]
    scratch += [pltpu.VMEM((4, hc, dim, dim), bf16) for _ in range(STEPS)]
    scratch += [pltpu.VMEM((SLOTS, hc, dim, dim), bf16) for _ in range(STEPS)]
    new_states, readout, mixed, flag = pl.pallas_call(
        routed_kernel,
        out_shape=(
            jax.ShapeDtypeStruct(states.shape, bf16),
            jax.ShapeDtypeStruct(qkv_rows.shape[1:], bf16),
            jax.ShapeDtypeStruct(hidden.shape, bf16),
            jax.ShapeDtypeStruct((8, 128), f32),
        ),
        in_specs=[hbm] * 10,
        out_specs=(hbm, vmem, vmem, vmem),
        scratch_shapes=scratch,
        compiler_params=pltpu.CompilerParams(
            collective_id=1, has_side_effects=True, vmem_limit_bytes=50 * 1024 * 1024
        ),
        cost_estimate=pl.CostEstimate(
            flops=6 * 16 * depth * units, bytes_accessed=6 * depth * units, transcendentals=0
        ),
    )(
        parents.T, decay_rate, expert_ids, gate_weights, qkv_rows, hidden, states,
        w_gate, w_up, w_down,
    )

    def again():
        return fused(
            states, qkv_rows, decay_rate, parents, hidden, expert_ids, gate_weights,
            w_gate, w_up, w_down,
        )

    return lax.cond(flag[0, 0] > 0.5, again, lambda: (new_states, readout, mixed))


def solution(mesh):
    in_specs = (
        P("expert", ("groups", "beam"), "head", None, None),
        P(None, "expert", ("groups", "beam"), "head", None),
        P("expert", ("groups", "beam"), "head"),
        P(None, ("groups", "beam")),
        P("expert", ("groups", "beam"), None),
        P("expert", "groups", None),
        P("expert", "groups", None),
        P("expert", None, ("beam", "head")),
        P("expert", None, ("beam", "head")),
        P("expert", ("beam", "head"), None),
    )
    out_specs = (
        P("expert", ("groups", "beam"), "head", None, None),
        P("expert", ("groups", "beam"), "head", None),
        P("expert", ("groups", "beam"), "head"),
    )
    sizes = mesh.shape
    fits = sizes["expert"] == 8 and sizes["beam"] == 2 and sizes["head"] == 1
    body = routed if fits else local
    return jax.shard_map(body, mesh=mesh, in_specs=in_specs, out_specs=out_specs, check_vma=False)
```

```python
import functools
import jax
import jax.numpy as jnp
from jax import lax
from jax.experimental import pallas as pl
from jax.experimental.pallas import tpu as pltpu
from jax.sharding import PartitionSpec as P


def local(
    states, qkv_rows, decay_rate, parents, hidden, expert_ids, gate_weights, w_gate, w_up, w_down
):
    beam_index = lax.axis_index("expert")
    parent_ids = lax.dynamic_index_in_dim(parents, beam_index, 0, keepdims=False)
    shard_piece = lax.all_gather(states, "expert", axis=0, tiled=True)
    source_ids = jnp.arange(shard_piece.shape[0], dtype=jnp.int32)
    matches = source_ids[:, None] == parent_ids[None, :]
    chosen = jnp.sum(
        jnp.where(matches[:, :, None, None, None], shard_piece, jnp.zeros((), jnp.bfloat16)), axis=0
    )
    query = qkv_rows[0, 0].astype(jnp.float32)
    key_part = qkv_rows[1, 0].astype(jnp.float32)
    value_part = qkv_rows[2, 0].astype(jnp.float32)
    updated = (
        decay_rate[0][..., None, None] * chosen.astype(jnp.float32)
        + key_part[..., :, None] * value_part[..., None, :]
    )
    new_states = updated.astype(jnp.bfloat16)[None]
    raw_out = jnp.einsum("rhk,rhkv->rhv", query, updated, precision=lax.Precision.HIGHEST)
    readout = (
        raw_out * lax.rsqrt(jnp.mean(raw_out * raw_out, axis=-1, keepdims=True) + 1e-05)
    ).astype(jnp.bfloat16)[None]
    beam_block = lax.all_gather(hidden, "beam", axis=1, tiled=True)[0]
    route_ids = expert_ids[0]
    route_gates = gate_weights[0]
    request_count = beam_block.shape[0]
    top_count = route_ids.shape[1]
    expert_count = lax.axis_size("expert") // 2
    capacity = min(request_count, 2 * request_count * top_count // expert_count)
    expert_range = jnp.arange(expert_count, dtype=jnp.int32)
    flat_ids = route_ids.reshape(-1)
    one_hot = (flat_ids[None, :] == expert_range[:, None]).astype(jnp.int32)
    slot_rank = jnp.cumsum(one_hot, axis=1) - 1
    slot_range = jnp.arange(capacity, dtype=jnp.int32)
    assignment = one_hot[:, :, None] * (slot_rank[:, :, None] == slot_range[None, None, :]).astype(
        jnp.int32
    )
    placement = assignment.reshape(expert_count, request_count, top_count, capacity).sum(axis=2)
    gate_select = jnp.sum(
        jnp.where(
            route_ids[None, :, :] == expert_range[:, None, None],
            route_gates[None, :, :],
            jnp.zeros((), jnp.float32),
        ),
        axis=2,
    )
    combine_weight = placement.astype(jnp.float32) * gate_select[:, :, None]
    dispatched = jnp.einsum(
        "xrc,rd->xcd",
        placement.astype(jnp.bfloat16),
        beam_block,
        preferred_element_type=jnp.float32,
    ).astype(jnp.bfloat16)
    outgoing = jnp.repeat(dispatched, 2, axis=0)
    arrived = lax.all_to_all(outgoing, "expert", split_axis=0, concat_axis=0, tiled=True)
    gate_val = jnp.einsum("scd,df->scf", arrived, w_gate[0], preferred_element_type=jnp.float32)
    up_val = jnp.einsum("scd,df->scf", arrived, w_up[0], preferred_element_type=jnp.float32)
    middle = (jax.nn.silu(gate_val) * up_val).astype(jnp.bfloat16)
    partial_value = jnp.einsum("scf,fd->scd", middle, w_down[0], preferred_element_type=jnp.float32)
    returned = lax.all_to_all(partial_value, "expert", split_axis=0, concat_axis=0, tiled=True)
    paired = returned.reshape(expert_count, 2, capacity, returned.shape[2]).sum(axis=1)
    partial_rows = jnp.einsum(
        "xrc,xcd->rd", combine_weight, paired, precision=lax.Precision.HIGHEST
    )
    beam_size = lax.axis_size("beam")
    head_size = lax.axis_size("head")
    local_rows = request_count // beam_size
    model_width = partial_rows.shape[1]
    arranged = partial_rows.reshape(beam_size, local_rows, head_size, model_width // head_size)
    arranged = arranged.transpose(0, 2, 1, 3).reshape(
        beam_size * head_size * local_rows, model_width // head_size
    )
    summed = lax.psum_scatter(arranged, ("beam", "head"), scatter_dimension=0, tiled=True)
    mixed = summed.astype(jnp.bfloat16).reshape(1, local_rows, model_width // head_size)
    return (new_states, readout, mixed)


CHUNKS = 8
PIECES = 4
SUB = 8


def fused_kernel(
    parents, decay, ids, gates, qkv, hid, states, w_gate, w_up, w_down,
    new_states, readout, mixed,
    row, rows, xb, gate_acc, up_acc, part, part_in, summed, final, raw,
    wg, wu, wd, picked, fresh,
    row_send, row_recv, block_send, block_recv, part_send, part_recv, sum_send, sum_recv,
    w_sem, own_sem, out_sem, st_send, st_recv, fwd_send, pick_send,
    *cand,
):
    e = lax.axis_index("expert")
    be = lax.axis_index("beam")
    z, c = e // 2, e % 2
    q = c * 2 + be
    side = z // 2
    inner = (z == 1) | (z == 2)
    outer = (z == 0) | (z == 3)
    sib = z * 2 + (1 - c)
    near = (1 + side) * 2 + c
    far = (2 - side) * 2 + c
    edge = 3 * side * 2 + c
    far_edge = 3 * (1 - side) * 2 + c
    chunks = len(cand)
    heads = qkv.shape[3]
    hc = heads // chunks
    width = row.shape[1]
    depth, hidden_units = w_gate.shape[1], w_gate.shape[2]
    f32 = jnp.float32

    def flip(index):
        return index + 1 - 2 * c

    def remote(src, dst, ssem, rsem, expert, beam):
        return pltpu.make_async_remote_copy(
            src_ref=src, dst_ref=dst, send_sem=ssem, recv_sem=rsem,
            device_id={"expert": expert, "beam": beam}, device_id_type=pl.DeviceIdType.MESH,
        )

    barrier = pltpu.get_barrier_semaphore()
    for step in range(1, 16):
        other = (e * 2 + be + step) % 16
        pl.semaphore_signal(
            barrier, inc=1, device_id={"expert": other // 2, "beam": other % 2},
            device_id_type=pl.DeviceIdType.MESH,
        )

    for p in range(PIECES):
        span = pl.ds(p * (depth // PIECES), depth // PIECES)
        pltpu.make_async_copy(w_gate.at[0, span], wg.at[span], w_sem.at[0, p]).start()
        pltpu.make_async_copy(w_up.at[0, span], wu.at[span], w_sem.at[1, p]).start()
    for p in range(PIECES):
        span = pl.ds(p * (hidden_units // PIECES), hidden_units // PIECES)
        pltpu.make_async_copy(w_down.at[0, span], wd.at[span], w_sem.at[2, p]).start()

    def own(k):
        return pltpu.make_async_copy(
            states.at[0, 0, pl.ds(k * hc, hc)], cand[k].at[e], own_sem.at[k]
        )

    for k in range(chunks):
        own(k).start()
    for j in range(SUB):
        row[j : j + 1, :] = hid[0, :, j * width : (j + 1) * width].astype(f32)
    rows[q, z] = row[...]
    pl.semaphore_wait(barrier, 15)

    def row_copy(step):
        there = (z + step) % 4
        return remote(
            row, rows.at[q, z], row_send.at[step - 1], row_recv.at[step - 1], there * 2 + c, be
        )

    def row_arrival(step):
        come = (z - step + 4) % 4
        return remote(
            row, rows.at[q, come], row_send.at[step - 1], row_recv.at[step - 1], come * 2 + c, be
        )

    for step in range(1, 4):
        row_copy(step).start()

    def state_copy(k, slot, expert):
        return remote(
            states.at[0, 0, pl.ds(k * hc, hc)], cand[k].at[e],
            st_send.at[k, slot], st_recv.at[k, e], expert, be,
        )

    def arrival(k, index):
        return remote(
            cand[k].at[index], cand[k].at[index], st_send.at[k, 0], st_recv.at[k, index], sib, be
        )

    def forward(k, slot, index):
        return remote(
            cand[k].at[index], cand[k].at[index],
            fwd_send.at[k, slot], st_recv.at[k, index], sib, be,
        )

    def pick_copy(k):
        return remote(
            picked.at[k], cand[k].at[8], pick_send.at[k], st_recv.at[k, 8], edge, be
        )

    for k in range(chunks):
        state_copy(k, 0, far).start()

        @pl.when(outer)
        def _():
            state_copy(k, 1, near).start()

        state_copy(k, 2, sib).start()

    for step in range(1, 4):
        row_arrival(step).wait_recv()

    def block_copy(step):
        to = (q + step) % 4
        return remote(
            rows.at[q], rows.at[q], block_send.at[step - 1], block_recv.at[step - 1],
            z * 2 + to // 2, to % 2,
        )

    def block_arrival(step):
        come = (q - step + 4) % 4
        return remote(
            rows.at[come], rows.at[come], block_send.at[step - 1], block_recv.at[step - 1],
            z * 2 + come // 2, come % 2,
        )

    for step in range(1, 4):
        block_copy(step).start()
    for step in range(1, 4):
        block_arrival(step).wait_recv()

    for j in range(SUB):
        xb[j] = rows[:, :, j, :].reshape(16, width).astype(jnp.bfloat16)
    gate_acc[...] = jnp.zeros_like(gate_acc)
    up_acc[...] = jnp.zeros_like(up_acc)
    per = SUB // PIECES

    @pl.loop(0, PIECES)
    def _(p):
        span = pl.ds(pl.multiple_of(p * (depth // PIECES), depth // PIECES), depth // PIECES)
        pltpu.make_async_copy(w_gate.at[0, span], wg.at[span], w_sem.at[0, p]).wait()
        pltpu.make_async_copy(w_up.at[0, span], wu.at[span], w_sem.at[1, p]).wait()
        for i in range(per):
            j = p * per + i
            cut = pl.ds(pl.multiple_of(j * width, width), width)
            gate_acc[...] += jnp.dot(xb[j], wg[cut, :], preferred_element_type=f32)
            up_acc[...] += jnp.dot(xb[j], wu[cut, :], preferred_element_type=f32)

    for p in range(PIECES):
        span = pl.ds(p * (hidden_units // PIECES), hidden_units // PIECES)
        pltpu.make_async_copy(w_down.at[0, span], wd.at[span], w_sem.at[2, p]).wait()
    gate_val = gate_acc[...]
    middle = (gate_val / (1.0 + jnp.exp(-gate_val)) * up_acc[...]).astype(jnp.bfloat16)
    for j in range(SUB):
        value = jnp.dot(
            middle, wd[:, j * width : (j + 1) * width], preferred_element_type=f32
        )
        part[:, :, j, :] = value.reshape(4, 4, width)

    def part_copy(step):
        to = (q + step) % 4
        return remote(
            part.at[to], part_in.at[step - 1], part_send.at[step - 1], part_recv.at[step - 1],
            z * 2 + to // 2, to % 2,
        )

    for step in range(1, 4):
        part_copy(step).start()

    flat = qkv[:, 0, 0].astype(f32).reshape(3 * heads, qkv.shape[4])
    padded = jnp.concatenate([flat, jnp.zeros((128 - 3 * heads, 128), f32)], axis=0)
    columns = padded.T
    values = qkv[2, 0, 0].astype(f32)

    def out_copy(k):
        return pltpu.make_async_copy(
            fresh.at[pl.ds(k * hc, hc)], new_states.at[0, 0, pl.ds(k * hc, hc)], out_sem.at[k]
        )

    def sum_copy(step):
        there = (z + step) % 4
        return remote(
            summed.at[there], final.at[z], sum_send.at[step - 1], sum_recv.at[step - 1],
            there * 2 + c, be,
        )

    def sum_arrival(step):
        come = (z - step + 4) % 4
        return remote(
            summed.at[come], final.at[come], sum_send.at[step - 1], sum_recv.at[step - 1],
            come * 2 + c, be,
        )

    mine = parents[e, 0]
    wanted = parents[edge, 0]
    index = jnp.where(inner | (mine // 2 == z), mine, 8)

    for k in range(chunks):
        own(k).wait()

        @pl.when(inner)
        def _():
            for slot, source in enumerate((edge, far, far_edge)):
                arrival(k, source).wait_recv()
                forward(k, slot, source).start()
            arrival(k, sib).wait_recv()
            for source in (edge, far, far_edge):
                arrival(k, flip(source)).wait_recv()
            picked[k] = cand[k][wanted]
            pick_copy(k).start()

        @pl.when(outer)
        def _():
            arrival(k, sib).wait_recv()
            arrival(k, 8).wait_recv()

        for h in range(hc):
            head = k * hc + h
            parent = cand[k][index, h].astype(f32)
            key = columns[:, heads + head : heads + head + 1]
            query = columns[:, head : head + 1]
            updated = decay[0, 0, head] * parent + key * values[head : head + 1, :]
            fresh[head] = updated.astype(jnp.bfloat16)
            raw[head : head + 1, :] = jnp.sum(query * updated, axis=0, keepdims=True)
        out_copy(k).start()

        if k == 0:
            for step in range(1, 4):
                part_copy(step).wait_recv()
            summed[...] = part[q] + part_in[0] + part_in[1] + part_in[2]
            for step in range(1, 4):
                sum_copy(step).start()
            final[z] = summed[z]

    raw_out = raw[...]
    scale = lax.rsqrt(jnp.mean(raw_out * raw_out, axis=-1, keepdims=True) + 1e-05)
    readout[0, 0] = (raw_out * scale).astype(jnp.bfloat16)

    for step in range(1, 4):
        sum_arrival(step).wait_recv()
    total = jnp.zeros((SUB, width), f32)
    for x in range(4):
        weight = jnp.float32(0.0)
        for t in range(ids.shape[2]):
            weight += jnp.where(ids[0, be, t] == x, gates[0, be, t], jnp.float32(0.0))
        total += weight * final[x]
    for j in range(SUB):
        mixed[0, :, j * width : (j + 1) * width] = total[j : j + 1, :].astype(jnp.bfloat16)

    for step in range(1, 4):
        row_copy(step).wait_send()
        block_copy(step).wait_send()
        part_copy(step).wait_send()
        sum_copy(step).wait_send()
    for k in range(chunks):
        out_copy(k).wait()
        state_copy(k, 0, far).wait_send()
        state_copy(k, 2, sib).wait_send()

        @pl.when(outer)
        def _():
            state_copy(k, 1, near).wait_send()

        @pl.when(inner)
        def _():
            for slot, source in enumerate((edge, far, far_edge)):
                forward(k, slot, source).wait_send()
            pick_copy(k).wait_send()


def fused(
    states, qkv_rows, decay_rate, parents, hidden, expert_ids, gate_weights, w_gate, w_up, w_down
):
    heads, dim = states.shape[2], states.shape[3]
    depth, units = w_gate.shape[1], w_gate.shape[2]
    width = depth // SUB
    hc = heads // CHUNKS
    f32, bf16 = jnp.float32, jnp.bfloat16
    smem = pl.BlockSpec(memory_space=pltpu.SMEM)
    vmem = pl.BlockSpec(memory_space=pltpu.VMEM)
    anywhere = pl.BlockSpec(memory_space=pl.ANY)
    dma = pltpu.SemaphoreType.DMA
    scratch = [
        pltpu.VMEM((SUB, width), f32),
        pltpu.VMEM((4, 4, SUB, width), f32),
        pltpu.VMEM((SUB, 16, width), bf16),
        pltpu.VMEM((16, units), f32),
        pltpu.VMEM((16, units), f32),
        pltpu.VMEM((4, 4, SUB, width), f32),
        pltpu.VMEM((3, 4, SUB, width), f32),
        pltpu.VMEM((4, SUB, width), f32),
        pltpu.VMEM((4, SUB, width), f32),
        pltpu.VMEM((heads, dim), f32),
        pltpu.VMEM((depth, units), bf16),
        pltpu.VMEM((depth, units), bf16),
        pltpu.VMEM((units, depth), bf16),
        pltpu.VMEM((CHUNKS, hc, dim, dim), bf16),
        pltpu.VMEM((heads, dim, dim), bf16),
        dma((3,)), dma((3,)), dma((3,)), dma((3,)), dma((3,)), dma((3,)), dma((3,)), dma((3,)),
        dma((3, PIECES)), dma((CHUNKS,)), dma((CHUNKS,)),
        dma((CHUNKS, 3)), dma((CHUNKS, 9)), dma((CHUNKS, 3)), dma((CHUNKS,)),
    ] + [pltpu.VMEM((9, hc, dim, dim), bf16) for _ in range(CHUNKS)]
    return pl.pallas_call(
        fused_kernel,
        out_shape=(
            jax.ShapeDtypeStruct(states.shape, bf16),
            jax.ShapeDtypeStruct(qkv_rows.shape[1:], bf16),
            jax.ShapeDtypeStruct(hidden.shape, bf16),
        ),
        in_specs=[smem] * 4 + [vmem] * 2 + [anywhere] * 4,
        out_specs=(anywhere, vmem, vmem),
        scratch_shapes=scratch,
        compiler_params=pltpu.CompilerParams(
            collective_id=0, has_side_effects=True, vmem_limit_bytes=50 * 1024 * 1024
        ),
        cost_estimate=pl.CostEstimate(
            flops=6 * 16 * depth * units, bytes_accessed=6 * depth * units, transcendentals=0
        ),
    )(
        parents, decay_rate, expert_ids, gate_weights, qkv_rows, hidden, states,
        w_gate, w_up, w_down,
    )


SLOTS = 3
AHEAD = 4
STEPS = 16


def routed_kernel(
    parents_in, decay_in, ids_in, gates_in, qkv_in, hid_in, states, w_gate, w_up, w_down,
    new_states, readout, mixed, flag,
    row, rows, xb, gate_acc, up_acc, middle, part, part_in, summed, final, raw,
    wg, wu, wd, picked, extra, edged, fresh, mark, marks,
    parents, decay, ids, gates, qkv, hid,
    small_sem, mark_send, mark_recv,
    row_send, row_recv, block_send, block_recv, part_send, part_recv, sum_send, sum_recv,
    w_sem, own_sem, out_sem, st_send, a_recv, b_recv, fwd_send, pick_send,
    *cand,
):
    steps = len(cand) // 2
    near_set, far_set = cand[:steps], cand[steps:]
    g = lax.axis_index("groups")
    e = lax.axis_index("expert")
    be = lax.axis_index("beam")
    z, c = e // 2, e % 2
    q = c * 2 + be
    side = z // 2
    inner = (z == 1) | (z == 2)
    outer = (z == 0) | (z == 3)
    sib = z * 2 + (1 - c)
    near = (1 + side) * 2 + c
    far = (2 - side) * 2 + c
    edge = 3 * side * 2 + c
    heads = qkv.shape[3]
    hc = heads // steps
    width = row.shape[1]
    depth, hidden_units = w_gate.shape[1], w_gate.shape[2]
    f32 = jnp.float32

    def remote(src, dst, ssem, rsem, expert, beam):
        return pltpu.make_async_remote_copy(
            src_ref=src, dst_ref=dst, send_sem=ssem, recv_sem=rsem,
            device_id={"expert": expert, "beam": beam}, device_id_type=pl.DeviceIdType.MESH,
        )

    small = [
        pltpu.make_async_copy(src, dst, small_sem.at[i])
        for i, (src, dst) in enumerate(
            (
                (hid_in, hid), (parents_in, parents), (qkv_in, qkv),
                (decay_in, decay), (ids_in, ids), (gates_in, gates),
            )
        )
    ]
    for copy in small:
        copy.start()

    barrier = pltpu.get_barrier_semaphore()
    for step in range(1, 16):
        other = (e * 2 + be + step) % 16
        pl.semaphore_signal(
            barrier, inc=1, device_id={"expert": other // 2, "beam": other % 2},
            device_id_type=pl.DeviceIdType.MESH,
        )
    for beam in range(2):
        pl.semaphore_signal(
            barrier, inc=1, device_id={"groups": 1 - g, "beam": beam},
            device_id_type=pl.DeviceIdType.MESH,
        )

    def own(k):
        return pltpu.make_async_copy(
            states.at[0, 0, pl.ds(k * hc, hc)], near_set[k].at[c], own_sem.at[k]
        )

    for k in range(steps):
        own(k).start()
    for p in range(PIECES):
        span = pl.ds(p * (depth // PIECES), depth // PIECES)
        pltpu.make_async_copy(w_gate.at[0, span], wg.at[span], w_sem.at[0, p]).start()
        pltpu.make_async_copy(w_up.at[0, span], wu.at[span], w_sem.at[1, p]).start()
    for p in range(PIECES):
        span = pl.ds(p * (hidden_units // PIECES), hidden_units // PIECES)
        pltpu.make_async_copy(w_down.at[0, span], wd.at[span], w_sem.at[2, p]).start()

    small[0].wait()
    for j in range(SUB):
        row[j : j + 1, :] = hid[0, :, j * width : (j + 1) * width].astype(f32)
    rows[q, z] = row[...]

    small[1].wait()
    zero, one = jnp.int32(0), jnp.int32(1)

    def needed(base, takers):
        found = []
        for j in range(4):
            hit = zero
            for i in range(4):
                hit = jnp.where(parents[0, takers + i] == base + j, one, hit)
            found.append(hit)
        return found

    my_base, other_base = 4 * side, 4 * (1 - side)
    going = needed(my_base, other_base)
    coming = needed(other_base, my_base)

    def rank_of(found, j):
        total = zero
        for i in range(4):
            total += jnp.where(i < j, found[i], zero)
        return jnp.minimum(total, SLOTS - 1)

    def entry_of(j):
        return (j & 1) + jnp.where(((j >> 1) & 1) == 1 - side, 0, 2)

    def chosen(slot):
        pick, before = zero, zero
        for j in range(4):
            pick = jnp.where((going[j] == 1) & (before == slot), jnp.int32(j), pick)
            before += going[j]
        return entry_of(pick)

    slot_entry = [chosen(slot) for slot in range(SLOTS)]
    my_slot = jnp.where(c == 0, slot_entry[0], slot_entry[1])
    overflow = (sum(going) > SLOTS) | (sum(coming) > SLOTS)
    mark[...] = jnp.zeros_like(mark) + jnp.where(overflow, f32(1.0), f32(0.0))

    wanted = parents[0, edge]
    edge_far = (wanted >> 2) != side
    edge_near_entry = entry_of(wanted & 3)
    edge_slot = rank_of(coming, wanted & 3)
    mine = parents[0, e]
    chip_own = (mine >> 1) == z
    use_far = jnp.where(inner, jnp.where((mine >> 2) != side, one, zero), jnp.where(chip_own, zero, one)) == 1
    near_entry = jnp.where(inner, entry_of(mine & 3), mine & 1)
    far_entry = jnp.where(inner, rank_of(coming, mine & 3), zero)

    pl.semaphore_wait(barrier, 17)

    def row_copy(step):
        there = (z + step) % 4
        return remote(
            row, rows.at[q, z], row_send.at[step - 1], row_recv.at[step - 1], there * 2 + c, be
        )

    def row_arrival(step):
        come = (z - step + 4) % 4
        return remote(
            row, rows.at[q, come], row_send.at[step - 1], row_recv.at[step - 1], come * 2 + c, be
        )

    def state_copy(k, slot, expert, entry):
        return remote(
            states.at[0, 0, pl.ds(k * hc, hc)], near_set[k].at[entry],
            st_send.at[k, slot], a_recv.at[k, entry], expert, be,
        )

    def near_arrival(k, entry):
        there = near_set[k].at[entry]
        return remote(there, there, st_send.at[k, 0], a_recv.at[k, entry], sib, be)

    def far_arrival(k, entry):
        there = far_set[k].at[entry]
        return remote(there, there, st_send.at[k, 0], b_recv.at[k, entry], sib, be)

    def near_forward(k):
        there = near_set[k].at[2 + c]
        return remote(there, there, fwd_send.at[k, 0], a_recv.at[k, 2 + c], sib, be)

    def far_forward(k, slot, entry):
        there = far_set[k].at[entry]
        return remote(there, there, fwd_send.at[k, slot], b_recv.at[k, entry], sib, be)

    def slot_copy(k):
        return remote(
            picked.at[k], far_set[k].at[c], pick_send.at[k, 0], b_recv.at[k, c], far, be
        )

    def extra_copy(k):
        return remote(
            extra.at[k // 2], far_set[k].at[2], pick_send.at[k, 1], b_recv.at[k, 2], far, be
        )

    def edge_copy(k):
        return remote(
            edged.at[k], far_set[k].at[0], pick_send.at[k, 2], b_recv.at[k, 0], edge, be
        )

    def send_own(k):
        @pl.when(outer)
        def _():
            state_copy(k, 1, near, 2 + c).start()

        state_copy(k, 0, sib, c).start()

    send_own(0)
    for step in range(1, 4):
        row_copy(step).start()
    for k in range(1, AHEAD):
        send_own(k)

    def mark_copy(step):
        column = (g * 2 + be + step) % 4
        return pltpu.make_async_remote_copy(
            src_ref=mark, dst_ref=marks.at[step - 1], send_sem=mark_send.at[step - 1],
            recv_sem=mark_recv.at[step - 1],
            device_id={"groups": column // 2, "beam": column % 2},
            device_id_type=pl.DeviceIdType.MESH,
        )

    def send_marks():
        for step in range(1, 4):
            mark_copy(step).start()

    def pass_near(k):
        @pl.when(inner)
        def _():
            near_arrival(k, 2 + c).wait_recv()
            near_forward(k).start()

    def send_slots(k):
        own(k).wait()
        near_arrival(k, 1 - c).wait_recv()

        @pl.when(inner)
        def _():
            near_arrival(k, 3 - c).wait_recv()
            picked[k] = near_set[k][my_slot]
            slot_copy(k).start()

        @pl.when(inner & (c == k % 2))
        def _():
            extra[k // 2] = near_set[k][slot_entry[2]]
            extra_copy(k).start()

    def pass_far(k):
        @pl.when(inner)
        def _():
            far_arrival(k, c).wait_recv()
            far_forward(k, 1, c).start()

        @pl.when(inner & (c == k % 2))
        def _():
            far_arrival(k, 2).wait_recv()
            far_forward(k, 2, 2).start()

    def out_copy(k):
        return pltpu.make_async_copy(
            fresh.at[pl.ds(k * hc, hc)], new_states.at[0, 0, pl.ds(k * hc, hc)], out_sem.at[k]
        )

    def send_edge(k):
        @pl.when(inner)
        def _():
            far_arrival(k, 1 - c).wait_recv()

        @pl.when(inner & (c != k % 2))
        def _():
            far_arrival(k, 2).wait_recv()

        @pl.when(inner)
        def _():
            edged[k] = jnp.where(edge_far, far_set[k][edge_slot], near_set[k][edge_near_entry])
            edge_copy(k).start()

    def finish(k):
        @pl.when(outer)
        def _():
            far_arrival(k, 0).wait_recv()

        for h in range(hc):
            head = k * hc + h
            parent = jnp.where(
                use_far, far_set[k][far_entry, h], near_set[k][near_entry, h]
            ).astype(f32)
            key = columns[:, heads + head : heads + head + 1]
            query = columns[:, head : head + 1]
            updated = decay[0, 0, head] * parent + key * values[head : head + 1, :]
            fresh[head] = updated.astype(jnp.bfloat16)
            raw[head : head + 1, :] = jnp.sum(query * updated, axis=0, keepdims=True)
        out_copy(k).start()

    def block_copy(step):
        to = (q + step) % 4
        return remote(
            rows.at[q], rows.at[q], block_send.at[step - 1], block_recv.at[step - 1],
            z * 2 + to // 2, to % 2,
        )

    def block_arrival(step):
        come = (q - step + 4) % 4
        return remote(
            rows.at[come], rows.at[come], block_send.at[step - 1], block_recv.at[step - 1],
            z * 2 + come // 2, come % 2,
        )

    def gather_first():
        for step in range(1, 4):
            row_arrival(step).wait_recv()
        for step in range(1, 4):
            block_copy(step).start()

    def gather_second():
        for step in range(1, 4):
            block_arrival(step).wait_recv()
        for j in range(SUB):
            xb[j] = rows[:, :, j, :].reshape(16, width).astype(jnp.bfloat16)
        gate_acc[...] = jnp.zeros_like(gate_acc)
        up_acc[...] = jnp.zeros_like(up_acc)

    per = SUB // PIECES

    def first_dots(p):
        span = pl.ds(p * (depth // PIECES), depth // PIECES)
        pltpu.make_async_copy(w_gate.at[0, span], wg.at[span], w_sem.at[0, p]).wait()
        pltpu.make_async_copy(w_up.at[0, span], wu.at[span], w_sem.at[1, p]).wait()
        for i in range(per):
            j = p * per + i
            cut = pl.ds(j * width, width)
            gate_acc[...] += jnp.dot(xb[j], wg[cut, :], preferred_element_type=f32)
            up_acc[...] += jnp.dot(xb[j], wu[cut, :], preferred_element_type=f32)

    def activate():
        for p in range(PIECES):
            span = pl.ds(p * (hidden_units // PIECES), hidden_units // PIECES)
            pltpu.make_async_copy(w_down.at[0, span], wd.at[span], w_sem.at[2, p]).wait()
        gate_val = gate_acc[...]
        middle[...] = (gate_val / (1.0 + jnp.exp(-gate_val)) * up_acc[...]).astype(jnp.bfloat16)

    def second_dots(p):
        for i in range(per):
            j = p * per + i
            value = jnp.dot(
                middle[...], wd[:, j * width : (j + 1) * width], preferred_element_type=f32
            )
            part[:, :, j, :] = value.reshape(4, 4, width)

    def part_copy(step):
        to = (q + step) % 4
        return remote(
            part.at[to], part_in.at[step - 1], part_send.at[step - 1], part_recv.at[step - 1],
            z * 2 + to // 2, to % 2,
        )

    def sum_copy(step):
        there = (z + step) % 4
        return remote(
            summed.at[there], final.at[z], sum_send.at[step - 1], sum_recv.at[step - 1],
            there * 2 + c, be,
        )

    def sum_arrival(step):
        come = (z - step + 4) % 4
        return remote(
            summed.at[come], final.at[come], sum_send.at[step - 1], sum_recv.at[step - 1],
            come * 2 + c, be,
        )

    def send_parts():
        for step in range(1, 4):
            part_copy(step).start()

    def send_sums():
        for step in range(1, 4):
            part_copy(step).wait_recv()
        summed[...] = part[q] + part_in[0] + part_in[1] + part_in[2]
        for step in range(1, 4):
            sum_copy(step).start()
        final[z] = summed[z]

    pass_near(0)
    for copy in small[2:]:
        copy.wait()
    flat = qkv[:, 0, 0].astype(f32).reshape(3 * heads, qkv.shape[4])
    padded = jnp.concatenate([flat, jnp.zeros((128 - 3 * heads, 128), f32)], axis=0)
    columns = padded.T
    values = qkv[2, 0, 0].astype(f32)

    work = [gather_first, gather_second, send_marks]
    work += [functools.partial(first_dots, p) for p in range(PIECES)]
    work += [activate]
    work += [functools.partial(second_dots, p) for p in range(PIECES)]
    work += [send_parts]
    share = -(-len(work) // steps)
    lag, last = 3, 4
    for i in range(steps + last):
        if i < steps:
            send_slots(i)
        if i + 1 < steps:
            pass_near(i + 1)
        if 0 <= i - lag < steps:
            pass_far(i - lag)
        if i + AHEAD < steps:
            send_own(i + AHEAD)
        for unit in work[i * share : (i + 1) * share]:
            unit()
        if 0 <= i - last < steps:
            send_edge(i - last)
            finish(i - last)
        if i == steps:
            send_sums()

    raw_out = raw[...]
    scale = lax.rsqrt(jnp.mean(raw_out * raw_out, axis=-1, keepdims=True) + 1e-05)
    readout[0, 0] = (raw_out * scale).astype(jnp.bfloat16)

    for step in range(1, 4):
        sum_arrival(step).wait_recv()
    total = jnp.zeros((SUB, width), f32)
    for x in range(4):
        weight = jnp.float32(0.0)
        for t in range(ids.shape[2]):
            weight += jnp.where(ids[0, be, t] == x, gates[0, be, t], jnp.float32(0.0))
        total += weight * final[x]
    for j in range(SUB):
        mixed[0, :, j * width : (j + 1) * width] = total[j : j + 1, :].astype(jnp.bfloat16)

    for step in range(1, 4):
        mark_copy(step).wait_recv()
    flag[...] = mark[...] + marks[0] + marks[1] + marks[2]

    for step in range(1, 4):
        mark_copy(step).wait_send()
        row_copy(step).wait_send()
        block_copy(step).wait_send()
        part_copy(step).wait_send()
        sum_copy(step).wait_send()
    for k in range(steps):
        out_copy(k).wait()
        state_copy(k, 0, sib, c).wait_send()

        @pl.when(outer)
        def _():
            state_copy(k, 1, near, 2 + c).wait_send()

        @pl.when(inner)
        def _():
            near_forward(k).wait_send()
            slot_copy(k).wait_send()
            far_forward(k, 1, c).wait_send()
            edge_copy(k).wait_send()

        @pl.when(inner & (c == k % 2))
        def _():
            extra_copy(k).wait_send()
            far_forward(k, 2, 2).wait_send()


def hand_on(a_in, b_in, c_in, a_out, b_out, c_out, sem):
    pairs = ((a_in, a_out), (b_in, b_out), (c_in, c_out))
    copies = [pltpu.make_async_copy(src, dst, sem.at[i]) for i, (src, dst) in enumerate(pairs)]
    for copy in copies:
        copy.start()
    for copy in copies:
        copy.wait()


def routed(
    states, qkv_rows, decay_rate, parents, hidden, expert_ids, gate_weights, w_gate, w_up, w_down
):
    heads, dim = states.shape[2], states.shape[3]
    depth, units = w_gate.shape[1], w_gate.shape[2]
    width = depth // SUB
    hc = heads // STEPS
    f32, bf16, i32 = jnp.float32, jnp.bfloat16, jnp.int32
    vmem = pl.BlockSpec(memory_space=pltpu.VMEM)
    hbm = pl.BlockSpec(memory_space=pltpu.HBM)
    dma = pltpu.SemaphoreType.DMA
    scratch = [
        pltpu.VMEM((SUB, width), f32),
        pltpu.VMEM((4, 4, SUB, width), f32),
        pltpu.VMEM((SUB, 16, width), bf16),
        pltpu.VMEM((16, units), f32),
        pltpu.VMEM((16, units), f32),
        pltpu.VMEM((16, units), bf16),
        pltpu.VMEM((4, 4, SUB, width), f32),
        pltpu.VMEM((3, 4, SUB, width), f32),
        pltpu.VMEM((4, SUB, width), f32),
        pltpu.VMEM((4, SUB, width), f32),
        pltpu.VMEM((heads, dim), f32),
        pltpu.VMEM((depth, units), bf16),
        pltpu.VMEM((depth, units), bf16),
        pltpu.VMEM((units, depth), bf16),
        pltpu.VMEM((STEPS, hc, dim, dim), bf16),
        pltpu.VMEM(((STEPS + 1) // 2, hc, dim, dim), bf16),
        pltpu.VMEM((STEPS, hc, dim, dim), bf16),
        pltpu.VMEM((heads, dim, dim), bf16),
        pltpu.VMEM((8, 128), f32),
        pltpu.VMEM((3, 8, 128), f32),
        pltpu.SMEM((1, parents.shape[0]), i32),
        pltpu.SMEM(decay_rate.shape, f32),
        pltpu.SMEM(expert_ids.shape, i32),
        pltpu.SMEM(gate_weights.shape, f32),
        pltpu.VMEM(qkv_rows.shape, bf16),
        pltpu.VMEM(hidden.shape, bf16),
        dma((6,)), dma((3,)), dma((3,)),
        dma((3,)), dma((3,)), dma((3,)), dma((3,)), dma((3,)), dma((3,)), dma((3,)), dma((3,)),
        dma((3, PIECES)), dma((STEPS,)), dma((STEPS,)),
        dma((STEPS, 2)), dma((STEPS, 4)), dma((STEPS, 3)), dma((STEPS, 3)), dma((STEPS, 3)),
    ]
    scratch += [pltpu.VMEM((4, hc, dim, dim), bf16) for _ in range(STEPS)]
    scratch += [pltpu.VMEM((SLOTS, hc, dim, dim), bf16) for _ in range(STEPS)]
    new_states, readout, mixed, flag = pl.pallas_call(
        routed_kernel,
        out_shape=(
            jax.ShapeDtypeStruct(states.shape, bf16),
            jax.ShapeDtypeStruct(qkv_rows.shape[1:], bf16),
            jax.ShapeDtypeStruct(hidden.shape, bf16),
            jax.ShapeDtypeStruct((8, 128), f32),
        ),
        in_specs=[hbm] * 10,
        out_specs=(hbm, vmem, vmem, vmem),
        scratch_shapes=scratch,
        compiler_params=pltpu.CompilerParams(
            collective_id=1, has_side_effects=True, vmem_limit_bytes=50 * 1024 * 1024
        ),
        cost_estimate=pl.CostEstimate(
            flops=6 * 16 * depth * units, bytes_accessed=6 * depth * units, transcendentals=0
        ),
    )(
        parents.T, decay_rate, expert_ids, gate_weights, qkv_rows, hidden, states,
        w_gate, w_up, w_down,
    )

    def again():
        return fused(
            states, qkv_rows, decay_rate, parents, hidden, expert_ids, gate_weights,
            w_gate, w_up, w_down,
        )

    outs = lax.cond(flag[0, 0] > 0.5, again, lambda: (new_states, readout, mixed))
    return tuple(
        pl.pallas_call(
            hand_on,
            out_shape=tuple(jax.ShapeDtypeStruct(x.shape, x.dtype) for x in outs),
            in_specs=[hbm] * 3,
            out_specs=(hbm,) * 3,
            scratch_shapes=[dma((3,))],
        )(*outs)
    )


def solution(mesh):
    in_specs = (
        P("expert", ("groups", "beam"), "head", None, None),
        P(None, "expert", ("groups", "beam"), "head", None),
        P("expert", ("groups", "beam"), "head"),
        P(None, ("groups", "beam")),
        P("expert", ("groups", "beam"), None),
        P("expert", "groups", None),
        P("expert", "groups", None),
        P("expert", None, ("beam", "head")),
        P("expert", None, ("beam", "head")),
        P("expert", ("beam", "head"), None),
    )
    out_specs = (
        P("expert", ("groups", "beam"), "head", None, None),
        P("expert", ("groups", "beam"), "head", None),
        P("expert", ("groups", "beam"), "head"),
    )
    sizes = mesh.shape
    fits = sizes["expert"] == 8 and sizes["beam"] == 2 and sizes["head"] == 1
    body = routed if fits else local
    return jax.shard_map(body, mesh=mesh, in_specs=in_specs, out_specs=out_specs, check_vma=False)
```
